32 devices in a mesh: groups: 2 (over y), tensor: 4 (over z), pool: 2 (over x), seq: 2 (over core).
Axes of the slice: x: 2, y: 2, z: 4, core: 2. Of those that a mesh axis runs over, the one named last changes fastest.
Arguments:
- prompt_states: bfloat16 [8, 512, 7168], P(('groups', 'pool', 'seq'), None, 'tensor'), parts along dimension 0, may hold values from -6 to 6
- kv_down: bfloat16 [7168, 576], P('tensor'), may hold values from -0.0625 to 0.0625
- kv_gain: float32 [512], replicated, may hold values from 0.1 to 1.9
- queries: bfloat16 [256, 4, 3072], P(('groups', 'pool'), None, 'tensor'), parts along dimension 0, may hold values from -8 to 8
- step_latents: bfloat16 [256, 4, 576], P(('groups', 'pool')), parts along dimension 0, may hold values from -8 to 8
- key_absorb: bfloat16 [16, 128, 512], P('tensor'), may hold values from -0.5 to 0.5
- value_absorb: bfloat16 [16, 512, 128], P('tensor'), may hold values from -0.875 to 0.875
- out_proj: bfloat16 [2048, 7168], P('tensor', ('pool', 'seq')), may hold values from -0.125 to 0.125
- cache_pages: bfloat16 [512, 128, 576], P(('groups', 'pool', 'seq')), parts along dimension 0, may hold values from -6 to 6
- page_table: int32 [256, 2, 1], P(('groups', 'pool'), 'seq'), parts along dimension 0, may hold values from 0 to 63, as said below
- cache_len: int32 [256], P('groups'), parts along dimension 0, may hold values from 1 to 256, as said below
- owner_map: int32 [256], P('groups'), parts along dimension 0, may hold values from 0 to 127, as said below
- senders: int32 [16], P('groups'), parts along dimension 0, may hold values from 0 to 127, as said below
- prompt_lens: int32 [16], P('groups'), parts along dimension 0, may hold values from 128 to 256, as said below
Outputs:
- new_latents: bfloat16 [8, 512, 576], P(('groups', 'pool', 'seq'), 'tensor'), parts along dimension 0
- attended: bfloat16 [256, 4, 7168], P(('groups', 'tensor'), None, ('pool', 'seq')), parts along dimension 0
The draws below stay inside these ranges and needn't reach their ends.
There are 2 independent parts, one for each index of `groups`. The reference program is written for one: setup_inputs(seed, part) draws one part's arguments, and reference() takes and returns one part's arrays. A program takes and returns all parts, laid end to end along the dimension named above; an argument that names none is the same for every part. Nothing has to cross between parts.
Inputs may be any that keep to these rules, and one draw needn't show every extreme that they name: `page_table`: for each pool and seq index, the entries of its rows and blocks are a permutation of 0 to 63. `cache_len`: some row holds the most. `owner_map`: each request once. Distinct request numbers; the two senders 2 g and 2 g + 1 of prompt group g are owned by decode rows of different pool indices, and each pool index owns 2 * 2 senders. `prompt_lens`: some sender fills its whole block.
All inputs are finite; a program needn't handle non-finite values.
Results may differ from the reference program's by a relative error of at most 0.013.
Values may be sent and summed in bfloat16 or wider, within the bound.
A program may use at most 128 MiB of HBM per device.

```python
import jax
import jax.numpy as jnp
from jax import lax

D = 7168
NOPE = 128
LAT = 512
VDIM = 128
PAGE = 128
STEPS = 4
ROW_DEV = 64
BLK_DEV = 1
PRE_DEV = 512
HEADS = 16
KVW = 576
QDIM = 192
ROWS = 128
PRE_GROUPS = 4
NEW_TOK = 2048
HALF = 256
SENDERS = 8
PAGES_DEV = 64
POOL_PAGES = 256
N_POOL = 2
N_SEQ = 2


def ownership(key):
    owner_map = jax.random.permutation(jax.random.fold_in(key, 501), ROWS).astype(jnp.int32)
    group_ids = jnp.arange(PRE_GROUPS, dtype=jnp.int32)
    offset = jax.random.randint(jax.random.fold_in(key, 502), (), 0, N_POOL)
    first_pool = (group_ids + offset) % N_POOL
    second_pool = (group_ids + offset + 1) % N_POOL
    pools = jnp.stack([first_pool, second_pool], axis=1).reshape(SENDERS)
    sender_ids = jnp.arange(SENDERS, dtype=jnp.int32)
    same_pool = pools[None, :] == pools[:, None]
    earlier = sender_ids[None, :] < sender_ids[:, None]
    rank = jnp.sum((same_pool & earlier).astype(jnp.int32), axis=1)
    perm_key = jax.random.fold_in(key, 503)
    orders = jax.vmap(lambda pool: jax.random.permutation(jax.random.fold_in(perm_key, pool), ROW_DEV))(jnp.arange(N_POOL))
    local_rows = orders[pools, rank]
    rows = pools * ROW_DEV + local_rows
    inverse = jnp.argsort(owner_map)
    senders = inverse[rows].astype(jnp.int32)
    return (owner_map, senders)


def draw_owner_map(key, part):
    owner_map, senders = ownership(key)
    return owner_map


def draw_senders(key, part):
    owner_map, senders = ownership(key)
    return senders


def draw_prompt_lens(key, part):
    own_key = jax.random.fold_in(key, 12)
    lengths = jax.random.randint(own_key, (SENDERS,), HALF // 2, HALF + 1)
    longest = jax.random.randint(jax.random.fold_in(own_key, 1), (), 0, SENDERS)
    return jnp.where(jnp.arange(SENDERS) == longest, HALF, lengths).astype(jnp.int32)


def draw_queries(key, part):
    own_key = jax.random.fold_in(key, 7)
    values = jnp.clip(jax.random.normal(own_key, (ROWS, STEPS, HEADS, QDIM)), -6.0, 6.0)
    return values.reshape(ROWS, STEPS, HEADS * QDIM).astype(jnp.bfloat16)


def draw_step_latents(key, part):
    own_key = jax.random.fold_in(key, 8)
    values = jnp.clip(jax.random.normal(own_key, (ROWS, STEPS, KVW)), -6.0, 6.0)
    return values.astype(jnp.bfloat16)


def draw_page_table(key, part):
    own_key = jax.random.fold_in(key, 9)
    member_ids = jnp.arange(N_POOL * N_SEQ)
    orders = jax.vmap(lambda member: jax.random.permutation(jax.random.fold_in(own_key, member), PAGES_DEV))(member_ids)
    orders = orders.reshape(N_POOL, N_SEQ, ROW_DEV, BLK_DEV).transpose(0, 2, 1, 3).reshape(ROWS, N_SEQ, BLK_DEV)
    return orders.astype(jnp.int32)


def draw_cache_len(key, part):
    own_key = jax.random.fold_in(key, 10)
    most_len = N_SEQ * BLK_DEV * PAGE
    lengths = jax.random.randint(own_key, (ROWS,), 1, most_len + 1)
    longest = jax.random.randint(jax.random.fold_in(own_key, 1), (), 0, ROWS)
    return jnp.where(jnp.arange(ROWS) == longest, most_len, lengths).astype(jnp.int32)


def level_of(rng, dims, shards, smallest, largest):
    def one(position, parts):
        heights = jax.random.uniform(jax.random.fold_in(jax.random.fold_in(rng, 6), position), (parts,), jnp.float32, smallest / len(shards), largest / len(shards))
        return jnp.repeat(jnp.exp(heights), dims[position] // parts).reshape((-1,) + (1,) * (len(dims) - position - 1))

    level = one(*shards[0])
    for cut in shards[1:]:
        level = level * one(*cut)
    return level


def gaussian(rng, extent, spread, limit, pieces=(), kind=jnp.bfloat16):
    values = spread * jax.random.normal(rng, extent, jnp.float32)
    if pieces:
        values = values * level_of(rng, extent, pieces, -0.22, 0.18)
    return jnp.clip(values, -limit, limit).astype(kind)


def setup_inputs(seed: int = 0, part: int = 0) -> dict:
    key_list = jax.random.split(jax.random.key(seed), 15)
    own_keys = jax.random.split(jax.random.fold_in(key_list[14], part), 15)
    return {
        "prompt_states": gaussian(own_keys[0], (PRE_GROUPS, PRE_DEV, D), 1.0, 6.0, ((0, 4), (2, 4))),
        "kv_down": gaussian(key_list[1], (D, KVW), D ** -0.5, 0.0625, ((0, 4),)),
        "kv_gain": jnp.clip(1.0 + 0.18 * jax.random.normal(key_list[2], (LAT,), jnp.float32), 0.1, 1.9),
        "queries": draw_queries(jax.random.fold_in(jax.random.fold_in(key_list[14], part), 71), part),
        "step_latents": draw_step_latents(jax.random.fold_in(jax.random.fold_in(key_list[14], part), 71), part),
        "key_absorb": gaussian(key_list[5], (HEADS, NOPE, LAT), NOPE ** -0.5, 0.5, ((0, 4),)),
        "value_absorb": gaussian(key_list[6], (HEADS, LAT, VDIM), 0.15, 0.875, ((0, 4),)),
        "out_proj": gaussian(key_list[7], (HEADS * VDIM, D), (HEADS * VDIM) ** -0.5, 0.125, ((0, 4), (1, 4))),
        "cache_pages": gaussian(own_keys[8], (POOL_PAGES, PAGE, KVW), 1.0, 6.0, ((0, 4),)),
        "page_table": draw_page_table(jax.random.fold_in(jax.random.fold_in(key_list[14], part), 71), part),
        "cache_len": draw_cache_len(jax.random.fold_in(jax.random.fold_in(key_list[14], part), 71), part),
        "owner_map": draw_owner_map(jax.random.fold_in(jax.random.fold_in(key_list[14], part), 71), part),
        "senders": draw_senders(jax.random.fold_in(jax.random.fold_in(key_list[14], part), 71), part),
        "prompt_lens": draw_prompt_lens(jax.random.fold_in(jax.random.fold_in(key_list[14], part), 71), part),
    }


EPSILON = 1e-06
THETA = 10000.0

def rows_meta(row_ids, owner_map, senders, cache_len):
    block_ids = (row_ids // HALF).astype(jnp.int32)
    offsets = (row_ids % HALF).astype(jnp.int32)
    request = senders[block_ids]
    target = owner_map[request]
    positions = offsets + cache_len[target]
    return (target, positions)

def finish_latents(summed, positions, kv_gain):
    lat_width = kv_gain.shape[0]
    latent_part = summed[:, :lat_width]
    rotary = summed[:, lat_width:]
    normed = latent_part * lax.rsqrt(lax.optimization_barrier(jnp.mean(latent_part * latent_part, axis=1, keepdims=True)) + EPSILON) * kv_gain[None, :]
    half_width = rotary.shape[1] // 2
    inv_freq = THETA ** (-(jnp.arange(half_width, dtype=jnp.float32) * 2.0 / rotary.shape[1]))
    angles = positions.astype(jnp.float32)[:, None] * inv_freq[None, :]
    cosine = jnp.cos(angles)
    sine_part = jnp.sin(angles)
    first_half = rotary[:, :half_width]
    second_half = rotary[:, half_width:]
    turned = jnp.concatenate([first_half * cosine - second_half * sine_part, first_half * sine_part + second_half * cosine], axis=1)
    return jnp.concatenate([normed, turned], axis=1).astype(jnp.bfloat16)

def reference(prompt_states, kv_down, kv_gain, queries, step_latents, key_absorb, value_absorb, out_proj, cache_pages, page_table, cache_len, owner_map, senders, prompt_lens):
    flat_states = prompt_states.reshape(NEW_TOK, D)
    summed = jnp.dot(flat_states, kv_down, preferred_element_type=jnp.float32)
    row_ids = jnp.arange(NEW_TOK, dtype=jnp.int32)
    target, positions = rows_meta(row_ids, owner_map, senders, cache_len)
    latents = finish_latents(summed, positions, kv_gain)
    new_latents = latents.reshape(N_POOL * N_SEQ, PRE_DEV, KVW)
    row_table = jnp.arange(ROWS, dtype=jnp.int32)
    sender_owner = owner_map[senders]
    hits = (sender_owner[None, :] == row_table[:, None]).astype(jnp.int32)
    row_length = lax.optimization_barrier(jnp.sum(hits * prompt_lens[None, :], axis=1))
    row_block = lax.optimization_barrier(jnp.sum(hits * jnp.arange(SENDERS, dtype=jnp.int32)[None, :], axis=1))
    slot_ids = jnp.arange(HALF, dtype=jnp.int32)
    new_index = (row_block[:, None] * HALF + slot_ids[None, :]).astype(jnp.int32)
    new_keys = latents[new_index]
    new_valid = slot_ids[None, :] < row_length[:, None]
    block_total = N_SEQ * BLK_DEV
    block_ids = jnp.arange(block_total, dtype=jnp.int32)
    seq_of = block_ids % N_SEQ
    local_of = block_ids // N_SEQ
    entries = page_table[:, seq_of, local_of]
    global_pages = (row_table[:, None] // ROW_DEV * N_SEQ + seq_of[None, :]) * PAGES_DEV + entries
    old_keys = cache_pages[global_pages.astype(jnp.int32)].reshape(ROWS, block_total * PAGE, KVW)
    old_valid = jnp.arange(block_total * PAGE, dtype=jnp.int32)[None, :] < cache_len[:, None]
    all_keys = jnp.concatenate([old_keys, new_keys, step_latents], axis=1)
    base_valid = jnp.concatenate([old_valid, new_valid], axis=1)
    step_ids = jnp.arange(STEPS, dtype=jnp.int32)
    step_valid = step_ids[None, :] <= step_ids[:, None]
    query_heads = queries.reshape(ROWS, STEPS, HEADS, QDIM)
    q_lat = jnp.einsum('rshn,hnl->rshl', query_heads[..., :NOPE].astype(jnp.float32), key_absorb.astype(jnp.float32)).astype(jnp.bfloat16)
    query_cat = jnp.concatenate([q_lat, query_heads[..., NOPE:]], axis=3)
    scale = float(QDIM) ** (-0.5)

    def one_row(operands):
        query_row, key_row, valid_row = operands
        valid = jnp.concatenate([jnp.broadcast_to(valid_row[None, :], (STEPS, valid_row.shape[0])), step_valid], axis=1)
        scores = jnp.einsum('shk,jk->shj', query_row.astype(jnp.float32), key_row.astype(jnp.float32)) * scale
        masked = jnp.where(valid[:, None, :], scores, -1e+30)
        top = lax.optimization_barrier(jnp.max(masked, axis=2, keepdims=True))
        weights = jnp.where(valid[:, None, :], jnp.exp(masked - top), 0.0)
        totals = lax.optimization_barrier(jnp.sum(weights, axis=2, keepdims=True))
        probs = weights.astype(jnp.bfloat16)
        mixed = jnp.einsum('shj,jl->shl', probs.astype(jnp.float32), key_row[:, :LAT].astype(jnp.float32))
        return (mixed / totals).astype(jnp.bfloat16)
    o_lat = lax.map(one_row, (query_cat, all_keys, base_valid))
    head_out = jnp.einsum('rshl,hlv->rshv', o_lat.astype(jnp.float32), value_absorb.astype(jnp.float32)).astype(jnp.bfloat16)
    head_out = head_out.reshape(ROWS * STEPS, HEADS * VDIM)
    attended = jnp.dot(head_out, out_proj, preferred_element_type=jnp.float32).astype(jnp.bfloat16).reshape(ROWS, STEPS, D)
    return (new_latents, attended)
```

```python
import jax
import jax.numpy as jnp
from jax import lax
from jax.experimental import pallas as pl
from jax.experimental.pallas import tpu as pltpu
from jax.sharding import PartitionSpec as P

EPSILON = 1e-06
THETA = 10000.0


def lookup(indices, table):
    table_ids = jnp.arange(table.shape[0], dtype=jnp.int32)
    matches = (indices[:, None] == table_ids[None, :]).astype(jnp.int32)
    return jnp.sum(matches * table[None, :], axis=1)


def rows_meta(row_ids, owner_map, senders, cache_len, half_rows):
    block_ids = row_ids // half_rows
    offsets = row_ids % half_rows
    request = lookup(block_ids, senders)
    target = lookup(request, owner_map)
    positions = offsets + lookup(target, cache_len)
    return (target, positions)


def finish_latents(summed, positions, kv_gain):
    lat_width = kv_gain.shape[0]
    latent_part = summed[:, :lat_width]
    rotary = summed[:, lat_width:]
    normed = (
        latent_part
        * lax.rsqrt(jnp.mean(latent_part * latent_part, axis=1, keepdims=True) + EPSILON)
        * kv_gain[None, :]
    )
    half_width = rotary.shape[1] // 2
    inv_freq = THETA ** (-(jnp.arange(half_width, dtype=jnp.float32) * 2.0 / rotary.shape[1]))
    angles = positions.astype(jnp.float32)[:, None] * inv_freq[None, :]
    cosine = jnp.cos(angles)
    sine_part = jnp.sin(angles)
    first_half = rotary[:, :half_width]
    second_half = rotary[:, half_width:]
    turned = jnp.concatenate(
        [
            first_half * cosine - second_half * sine_part,
            first_half * sine_part + second_half * cosine,
        ],
        axis=1,
    )
    return jnp.concatenate([normed, turned], axis=1).astype(jnp.bfloat16)


MESH = pl.DeviceIdType.MESH


def tail_kernel(
    o_ref,
    lse_ref,
    absorb_ref,
    proj_ref,
    out_ref,
    o_in,
    lse_in,
    heads,
    up,
    down,
    total_ref,
    pair_send,
    pair_recv,
    gather_send,
    gather_recv,
    forward_send,
    forward_recv,
    up_send,
    up_recv,
    down_send,
    down_recv,
):
    tensor_count = lax.axis_size("tensor")
    pool_count = lax.axis_size("pool")
    depth = lax.axis_index("tensor")
    pool = lax.axis_index("pool")
    seq = lax.axis_index("seq")
    head_count, half, _ = o_ref.shape[1:]
    value_width = absorb_ref.shape[2]
    chunk = out_ref.shape[0]
    other = 1 - seq
    has_below = depth > 0
    has_above = depth < tensor_count - 1

    barrier = pltpu.get_barrier_semaphore()
    pl.semaphore_signal(barrier, inc=1, device_id={"seq": other}, device_id_type=MESH)
    for step in range(1, pool_count):
        pl.semaphore_signal(
            barrier,
            inc=1,
            device_id={"pool": lax.rem(pool + step, pool_count)},
            device_id_type=MESH,
        )

    @pl.when(has_below)
    def _():
        pl.semaphore_signal(barrier, inc=1, device_id={"tensor": depth - 1}, device_id_type=MESH)

    @pl.when(has_above)
    def _():
        pl.semaphore_signal(barrier, inc=1, device_id={"tensor": depth + 1}, device_id_type=MESH)

    pl.semaphore_wait(
        barrier, pool_count + has_below.astype(jnp.int32) + has_above.astype(jnp.int32)
    )

    pair = [
        pltpu.make_async_remote_copy(
            src_ref=lse_ref.at[other],
            dst_ref=lse_in,
            send_sem=pair_send.at[0],
            recv_sem=pair_recv.at[0],
            device_id={"seq": other},
            device_id_type=MESH,
        )
    ] + [
        pltpu.make_async_remote_copy(
            src_ref=o_ref.at[other, h],
            dst_ref=o_in.at[h],
            send_sem=pair_send.at[1 + h],
            recv_sem=pair_recv.at[1 + h],
            device_id={"seq": other},
            device_id_type=MESH,
        )
        for h in range(head_count)
    ]
    for copy in pair:
        copy.start()
    own_rows = pl.ds(pl.multiple_of((pool * 2 + seq) * half, half), half)
    pair[0].wait_recv()
    for h in range(head_count):
        pair[1 + h].wait_recv()
        mine = lse_ref[seq, h][:, :1]
        theirs = lse_in[h][:, :1]
        ratio = 1.0 / (1.0 + jnp.exp(jnp.clip(theirs - mine, -80.0, 80.0)))
        merged = o_ref[seq, h].astype(jnp.float32) * ratio + o_in[h].astype(jnp.float32) * (
            1.0 - ratio
        )
        heads[own_rows, h * value_width : (h + 1) * value_width] = jnp.dot(
            merged.astype(jnp.bfloat16), absorb_ref[h], preferred_element_type=jnp.float32
        ).astype(jnp.bfloat16)

    def rows_of(pool_id, seq_id):
        return pl.ds(pl.multiple_of((pool_id * 2 + seq_id) * half, half), half)

    gathers = []
    for step in range(1, pool_count):
        gathers.append(
            pltpu.make_async_remote_copy(
                src_ref=heads.at[own_rows],
                dst_ref=heads.at[own_rows],
                send_sem=gather_send.at[step],
                recv_sem=gather_recv.at[step],
                device_id={"pool": lax.rem(pool + step, pool_count)},
                device_id_type=MESH,
            )
        )
    forwards = []
    for step in range(pool_count):
        rows = rows_of(lax.rem(pool + pool_count - step, pool_count), seq)
        forwards.append(
            pltpu.make_async_remote_copy(
                src_ref=heads.at[rows],
                dst_ref=heads.at[rows],
                send_sem=forward_send.at[step],
                recv_sem=forward_recv.at[step],
                device_id={"seq": other},
                device_id_type=MESH,
            )
        )
    for copy in gathers:
        copy.start()
    forwards[0].start()
    for step in range(1, pool_count):
        gathers[step - 1].wait_recv()
        forwards[step].start()
    for copy in forwards:
        copy.wait_recv()

    def project(dest):
        rows = pl.ds(pl.multiple_of(dest * chunk, chunk), chunk)
        return jnp.dot(heads[rows, :], proj_ref[...], preferred_element_type=jnp.float32)

    def lane_copy(buffer, send, recv, dest, target):
        return pltpu.make_async_remote_copy(
            src_ref=buffer.at[dest],
            dst_ref=buffer.at[dest],
            send_sem=send.at[dest],
            recv_sem=recv.at[dest],
            device_id={"tensor": target},
            device_id_type=MESH,
        )

    def pass_on(buffer, send, recv, dest, target, has_source):
        part = project(dest)
        copy = lane_copy(buffer, send, recv, dest, target)

        @pl.when(has_source)
        def _():
            copy.wait_recv()
            buffer[dest] = (buffer[dest].astype(jnp.float32) + part).astype(jnp.bfloat16)

        @pl.when(jnp.logical_not(has_source))
        def _():
            buffer[dest] = part.astype(jnp.bfloat16)

        copy.start()

    def turn(step, carry):
        high = tensor_count - 1 - step

        @pl.when(high > depth)
        def _():
            pass_on(up, up_send, up_recv, high, depth + 1, has_below)

        @pl.when(step < depth)
        def _():
            pass_on(down, down_send, down_recv, step, depth - 1, has_above)

        return carry

    lax.fori_loop(0, tensor_count - 1, turn, 0)
    total = project(depth)

    total_ref[...] = total

    @pl.when(has_below)
    def _():
        lane_copy(up, up_send, up_recv, depth, depth - 1).wait_recv()
        total_ref[...] += up[depth].astype(jnp.float32)

    @pl.when(has_above)
    def _():
        lane_copy(down, down_send, down_recv, depth, depth + 1).wait_recv()
        total_ref[...] += down[depth].astype(jnp.float32)

    out_ref[...] = total_ref[...].astype(jnp.bfloat16)

    def drain(step, carry):
        high = tensor_count - 1 - step

        @pl.when(high > depth)
        def _():
            lane_copy(up, up_send, up_recv, high, depth + 1).wait_send()

        @pl.when(step < depth)
        def _():
            lane_copy(down, down_send, down_recv, step, depth - 1).wait_send()

        return carry

    lax.fori_loop(0, tensor_count - 1, drain, 0)
    for copy in pair + gathers + forwards:
        copy.wait_send()


def tail(o_parts, lse, value_absorb, out_proj):
    tensor_count = lax.axis_size("tensor")
    pool_count = lax.axis_size("pool")
    _, head_count, half, lat_width = o_parts.shape
    columns = out_proj.shape[1]
    total_rows = pool_count * 2 * half
    chunk = total_rows // tensor_count
    vmem = pl.BlockSpec(memory_space=pltpu.VMEM)
    dma = pltpu.SemaphoreType.DMA
    return pl.pallas_call(
        tail_kernel,
        out_shape=jax.ShapeDtypeStruct((chunk, columns), jnp.bfloat16),
        in_specs=[vmem] * 4,
        out_specs=vmem,
        scratch_shapes=[
            pltpu.VMEM((head_count, half, lat_width), jnp.bfloat16),
            pltpu.VMEM((head_count, half, 128), jnp.float32),
            pltpu.VMEM((total_rows, out_proj.shape[0]), jnp.bfloat16),
            pltpu.VMEM((tensor_count, chunk, columns), jnp.bfloat16),
            pltpu.VMEM((tensor_count, chunk, columns), jnp.bfloat16),
            pltpu.VMEM((chunk, columns), jnp.float32),
            dma((1 + head_count,)),
            dma((1 + head_count,)),
            dma((pool_count,)),
            dma((pool_count,)),
            dma((pool_count,)),
            dma((pool_count,)),
            dma((tensor_count,)),
            dma((tensor_count,)),
            dma((tensor_count,)),
            dma((tensor_count,)),
        ],
        compiler_params=pltpu.CompilerParams(
            collective_id=0, has_side_effects=True, vmem_limit_bytes=40 * 1024 * 1024
        ),
        name="tail",
    )(o_parts, lse, value_absorb, out_proj)


def local(
    prompt_states,
    kv_down,
    kv_gain,
    queries,
    step_latents,
    key_absorb,
    value_absorb,
    out_proj,
    cache_pages,
    page_table,
    cache_len,
    owner_map,
    senders,
    prompt_lens,
):
    tensor_count = lax.axis_size("tensor")
    pool_count = lax.axis_size("pool")
    seq_count = lax.axis_size("seq")
    pool_index = lax.axis_index("pool")
    seq_index = lax.axis_index("seq")
    tensor_index = lax.axis_index("tensor")
    pre_rows = prompt_states.shape[1]
    half_rows = pre_rows // 2
    share_rows = pre_rows // tensor_count
    row_count = queries.shape[0]
    group_index = pool_index * seq_count + seq_index
    group_start = group_index * pre_rows
    partial_sum = jnp.dot(prompt_states[0], kv_down, preferred_element_type=jnp.float32)
    summed = lax.psum(partial_sum.astype(jnp.bfloat16), "tensor").astype(jnp.float32)
    row_ids = group_start + jnp.arange(pre_rows, dtype=jnp.int32)
    target, positions = rows_meta(row_ids, owner_map, senders, cache_len, half_rows)
    latents = finish_latents(summed, positions, kv_gain)
    new_latents = lax.dynamic_slice_in_dim(latents, tensor_index * share_rows, share_rows, 0)[None]
    own_senders = 2 * group_index + jnp.arange(2, dtype=jnp.int32)
    own_targets = lookup(lookup(own_senders, senders), owner_map)
    own_lengths = lookup(own_senders, prompt_lens)
    target_pools = own_targets // row_count
    target_rows = own_targets % row_count
    pool_ids = jnp.arange(pool_count, dtype=jnp.int32)
    is_first = pool_ids == target_pools[0]
    is_second = pool_ids == target_pools[1]
    first_block = latents[:half_rows]
    second_block = latents[half_rows:]
    outgoing = jnp.where(
        is_first[:, None, None],
        first_block[None],
        jnp.where(is_second[:, None, None], second_block[None], jnp.zeros((), jnp.bfloat16)),
    )
    labels = jnp.where(is_first, target_rows[0], jnp.where(is_second, target_rows[1], -1))
    lengths = jnp.where(is_first, own_lengths[0], jnp.where(is_second, own_lengths[1], 0))
    meta = jnp.stack([labels, lengths], axis=1)
    arrived, arrived_meta = (
        lax.all_to_all(outgoing, "pool", split_axis=0, concat_axis=0, tiled=True),
        lax.all_to_all(meta, "pool", split_axis=0, concat_axis=0, tiled=True),
    )
    lat_width = kv_gain.shape[0]
    head_count = key_absorb.shape[0]
    nope_width = key_absorb.shape[1]
    step_count = queries.shape[1]
    query_width = queries.shape[2] // head_count
    query_heads = queries.reshape(row_count, step_count, head_count, query_width)
    q_lat = jnp.einsum(
        "rshn,hnl->rshl",
        query_heads[..., :nope_width],
        key_absorb,
        preferred_element_type=jnp.float32,
    ).astype(jnp.bfloat16)
    query_cat = jnp.concatenate([q_lat, query_heads[..., nope_width:]], axis=3)
    scale = float(query_width) ** (-0.5)
    local_len = lax.dynamic_slice_in_dim(cache_len, pool_index * row_count, row_count, 0)
    page_ids = page_table[:, 0, :]
    block_count = page_ids.shape[1]
    page_len = cache_pages.shape[1]
    old_keys = cache_pages[page_ids].reshape(
        row_count, block_count * page_len, cache_pages.shape[2]
    )
    token_ids = jnp.arange(block_count * page_len, dtype=jnp.int32)
    old_positions = (
        token_ids // page_len * seq_count + seq_index
    ) * page_len + token_ids % page_len
    row_ids_local = jnp.arange(row_count, dtype=jnp.int32)
    old_mask = (old_positions[None, :] < local_len[:, None])[:, None, None, :]
    step_ids = jnp.arange(step_count, dtype=jnp.int32)
    own_mask = ((step_ids[None, :] <= step_ids[:, None]) & (seq_index == 0))[None, :, None, :]
    block_labels = arrived_meta[:, 0]
    block_lengths = arrived_meta[:, 1]
    safe_labels = jnp.maximum(block_labels, 0)
    block_queries = query_cat[safe_labels]
    slot_ids = jnp.arange(arrived.shape[1], dtype=jnp.int32)
    block_mask = (slot_ids[None, :] < block_lengths[:, None])[:, None, None, :]
    owned = block_labels[None, :] == row_ids_local[:, None]
    old_scores = (
        jnp.einsum("rshk,rjk->rshj", query_cat, old_keys, preferred_element_type=jnp.float32)
        * scale
    )
    new_scores = (
        jnp.einsum("bshk,bjk->bshj", block_queries, arrived, preferred_element_type=jnp.float32)
        * scale
    )
    own_scores = (
        jnp.einsum("rshk,rtk->rsht", query_cat, step_latents, preferred_element_type=jnp.float32)
        * scale
    )
    old_masked = jnp.where(old_mask, old_scores, -1e30)
    new_masked = jnp.where(block_mask, new_scores, -1e30)
    own_masked = jnp.where(own_mask, own_scores, -1e30)
    block_top = jnp.max(new_masked, axis=3)
    row_new_top = jnp.max(jnp.where(owned[:, :, None, None], block_top[None], -1e30), axis=1)
    local_top = jnp.maximum(
        jnp.maximum(jnp.max(old_masked, axis=3), row_new_top), jnp.max(own_masked, axis=3)
    )
    top = local_top
    block_ceiling = top[safe_labels]
    old_weights = jnp.where(old_mask, jnp.exp(old_masked - top[..., None]), 0.0)
    new_weights = jnp.where(block_mask, jnp.exp(new_masked - block_ceiling[..., None]), 0.0)
    own_weights = jnp.where(own_mask, jnp.exp(own_masked - top[..., None]), 0.0)
    owned_float = owned.astype(jnp.float32)
    block_totals = jnp.sum(new_weights, axis=3)
    block_mixed = jnp.einsum(
        "bshj,bjl->bshl",
        new_weights.astype(jnp.bfloat16),
        arrived[..., :lat_width],
        preferred_element_type=jnp.float32,
    )
    totals = jnp.sum(old_weights, axis=3) + jnp.sum(own_weights, axis=3)
    totals = totals + jnp.einsum(
        "rb,bsh->rsh", owned_float, block_totals, precision=lax.Precision.HIGHEST
    )
    mixed = jnp.einsum(
        "rshj,rjl->rshl",
        old_weights.astype(jnp.bfloat16),
        old_keys[..., :lat_width],
        preferred_element_type=jnp.float32,
    )
    mixed = mixed + jnp.einsum(
        "rsht,rtl->rshl",
        own_weights.astype(jnp.bfloat16),
        step_latents[..., :lat_width],
        preferred_element_type=jnp.float32,
    )
    mixed = mixed + jnp.einsum(
        "rb,bshl->rshl", owned_float, block_mixed, precision=lax.Precision.HIGHEST
    )
    positive = totals > 0.0
    safe_totals = jnp.where(positive, totals, 1.0)
    o_part = (mixed / safe_totals[..., None]).astype(jnp.bfloat16)
    lse = jnp.where(positive, top + jnp.log(safe_totals), -1e30)
    half = row_count * step_count // 2
    o_parts = o_part.transpose(2, 0, 1, 3).reshape(head_count, 2, half, lat_width)
    lse_parts = lse.transpose(2, 0, 1).reshape(head_count, 2, half)
    attended = tail(
        o_parts.transpose(1, 0, 2, 3),
        jnp.broadcast_to(lse_parts.transpose(1, 0, 2)[..., None], (2, head_count, half, 128)),
        value_absorb,
        out_proj,
    ).reshape(-1, step_count, out_proj.shape[1])
    return (new_latents, attended)


def solution(mesh):
    placed = (
        P(("groups", "pool", "seq"), None, "tensor"),
        P("tensor", None),
        P(),
        P(("groups", "pool"), None, "tensor"),
        P(("groups", "pool"), None, None),
        P("tensor", None, None),
        P("tensor", None, None),
        P("tensor", ("pool", "seq")),
        P(("groups", "pool", "seq"), None, None),
        P(("groups", "pool"), "seq", None),
        P("groups"),
        P("groups"),
        P("groups"),
        P("groups"),
    )
    return jax.shard_map(
        local,
        mesh=mesh,
        in_specs=placed,
        out_specs=(
            P(("groups", "pool", "seq"), "tensor", None),
            P(("groups", "tensor"), None, ("pool", "seq")),
        ),
        check_vma=False,
    )
```

```python
import functools

import jax
import jax.numpy as jnp
from jax import lax
from jax.experimental import pallas as pl
from jax.experimental.pallas import tpu as pltpu
from jax.sharding import PartitionSpec as P

EPSILON = 1e-06
THETA = 10000.0


def lookup(indices, table):
    table_ids = jnp.arange(table.shape[0], dtype=jnp.int32)
    matches = (indices[:, None] == table_ids[None, :]).astype(jnp.int32)
    return jnp.sum(matches * table[None, :], axis=1)


def rows_meta(row_ids, owner_map, senders, cache_len, half_rows):
    block_ids = row_ids // half_rows
    offsets = row_ids % half_rows
    request = lookup(block_ids, senders)
    target = lookup(request, owner_map)
    positions = offsets + lookup(target, cache_len)
    return (target, positions)


MESH = pl.DeviceIdType.MESH


def tail_kernel(
    o_ref,
    lse_ref,
    absorb_ref,
    proj_ref,
    out_ref,
    o_in,
    lse_in,
    heads,
    up,
    down,
    total_ref,
    pair_send,
    pair_recv,
    gather_send,
    gather_recv,
    forward_send,
    forward_recv,
    up_send,
    up_recv,
    down_send,
    down_recv,
):
    tensor_count = lax.axis_size("tensor")
    pool_count = lax.axis_size("pool")
    depth = lax.axis_index("tensor")
    pool = lax.axis_index("pool")
    seq = lax.axis_index("seq")
    head_count, half, _ = o_ref.shape[1:]
    value_width = absorb_ref.shape[2]
    chunk = out_ref.shape[0]
    other = 1 - seq
    has_below = depth > 0
    has_above = depth < tensor_count - 1

    barrier = pltpu.get_barrier_semaphore()
    pl.semaphore_signal(barrier, inc=1, device_id={"seq": other}, device_id_type=MESH)
    for step in range(1, pool_count):
        pl.semaphore_signal(
            barrier,
            inc=1,
            device_id={"pool": lax.rem(pool + step, pool_count)},
            device_id_type=MESH,
        )

    @pl.when(has_below)
    def _():
        pl.semaphore_signal(barrier, inc=1, device_id={"tensor": depth - 1}, device_id_type=MESH)

    @pl.when(has_above)
    def _():
        pl.semaphore_signal(barrier, inc=1, device_id={"tensor": depth + 1}, device_id_type=MESH)

    pl.semaphore_wait(
        barrier, pool_count + has_below.astype(jnp.int32) + has_above.astype(jnp.int32)
    )

    pair = [
        pltpu.make_async_remote_copy(
            src_ref=lse_ref.at[other],
            dst_ref=lse_in,
            send_sem=pair_send.at[0],
            recv_sem=pair_recv.at[0],
            device_id={"seq": other},
            device_id_type=MESH,
        )
    ] + [
        pltpu.make_async_remote_copy(
            src_ref=o_ref.at[other, h],
            dst_ref=o_in.at[h],
            send_sem=pair_send.at[1 + h],
            recv_sem=pair_recv.at[1 + h],
            device_id={"seq": other},
            device_id_type=MESH,
        )
        for h in range(head_count)
    ]
    for copy in pair:
        copy.start()
    own_rows = pl.ds(pl.multiple_of((pool * 2 + seq) * half, half), half)
    pair[0].wait_recv()
    for h in range(head_count):
        pair[1 + h].wait_recv()
        mine = lse_ref[seq, h][:, :1]
        theirs = lse_in[h][:, :1]
        ratio = 1.0 / (1.0 + jnp.exp(jnp.clip(theirs - mine, -80.0, 80.0)))
        merged = o_ref[seq, h].astype(jnp.float32) * ratio + o_in[h].astype(jnp.float32) * (
            1.0 - ratio
        )
        heads[own_rows, h * value_width : (h + 1) * value_width] = jnp.dot(
            merged.astype(jnp.bfloat16), absorb_ref[h], preferred_element_type=jnp.float32
        ).astype(jnp.bfloat16)

    def rows_of(pool_id, seq_id):
        return pl.ds(pl.multiple_of((pool_id * 2 + seq_id) * half, half), half)

    gathers = []
    for step in range(1, pool_count):
        gathers.append(
            pltpu.make_async_remote_copy(
                src_ref=heads.at[own_rows],
                dst_ref=heads.at[own_rows],
                send_sem=gather_send.at[step],
                recv_sem=gather_recv.at[step],
                device_id={"pool": lax.rem(pool + step, pool_count)},
                device_id_type=MESH,
            )
        )
    forwards = []
    for step in range(pool_count):
        rows = rows_of(lax.rem(pool + pool_count - step, pool_count), seq)
        forwards.append(
            pltpu.make_async_remote_copy(
                src_ref=heads.at[rows],
                dst_ref=heads.at[rows],
                send_sem=forward_send.at[step],
                recv_sem=forward_recv.at[step],
                device_id={"seq": other},
                device_id_type=MESH,
            )
        )
    for copy in gathers:
        copy.start()
    forwards[0].start()
    for step in range(1, pool_count):
        gathers[step - 1].wait_recv()
        forwards[step].start()
    for copy in forwards:
        copy.wait_recv()

    def project(dest):
        rows = pl.ds(pl.multiple_of(dest * chunk, chunk), chunk)
        return jnp.dot(heads[rows, :], proj_ref[...], preferred_element_type=jnp.float32)

    def lane_copy(buffer, send, recv, dest, target):
        return pltpu.make_async_remote_copy(
            src_ref=buffer.at[dest],
            dst_ref=buffer.at[dest],
            send_sem=send.at[dest],
            recv_sem=recv.at[dest],
            device_id={"tensor": target},
            device_id_type=MESH,
        )

    def pass_on(buffer, send, recv, dest, target, has_source):
        part = project(dest)
        copy = lane_copy(buffer, send, recv, dest, target)

        @pl.when(has_source)
        def _():
            copy.wait_recv()
            buffer[dest] = (buffer[dest].astype(jnp.float32) + part).astype(jnp.bfloat16)

        @pl.when(jnp.logical_not(has_source))
        def _():
            buffer[dest] = part.astype(jnp.bfloat16)

        copy.start()

    def turn(step, carry):
        high = tensor_count - 1 - step

        @pl.when(high > depth)
        def _():
            pass_on(up, up_send, up_recv, high, depth + 1, has_below)

        @pl.when(step < depth)
        def _():
            pass_on(down, down_send, down_recv, step, depth - 1, has_above)

        return carry

    lax.fori_loop(0, tensor_count - 1, turn, 0)
    total = project(depth)

    total_ref[...] = total

    @pl.when(has_below)
    def _():
        lane_copy(up, up_send, up_recv, depth, depth - 1).wait_recv()
        total_ref[...] += up[depth].astype(jnp.float32)

    @pl.when(has_above)
    def _():
        lane_copy(down, down_send, down_recv, depth, depth + 1).wait_recv()
        total_ref[...] += down[depth].astype(jnp.float32)

    out_ref[...] = total_ref[...].astype(jnp.bfloat16)

    def drain(step, carry):
        high = tensor_count - 1 - step

        @pl.when(high > depth)
        def _():
            lane_copy(up, up_send, up_recv, high, depth + 1).wait_send()

        @pl.when(step < depth)
        def _():
            lane_copy(down, down_send, down_recv, step, depth - 1).wait_send()

        return carry

    lax.fori_loop(0, tensor_count - 1, drain, 0)
    for copy in pair + gathers + forwards:
        copy.wait_send()


def tail(o_parts, lse, value_absorb, out_proj):
    tensor_count = lax.axis_size("tensor")
    pool_count = lax.axis_size("pool")
    _, head_count, half, lat_width = o_parts.shape
    columns = out_proj.shape[1]
    total_rows = pool_count * 2 * half
    chunk = total_rows // tensor_count
    vmem = pl.BlockSpec(memory_space=pltpu.VMEM)
    dma = pltpu.SemaphoreType.DMA
    return pl.pallas_call(
        tail_kernel,
        out_shape=jax.ShapeDtypeStruct((chunk, columns), jnp.bfloat16),
        in_specs=[vmem] * 4,
        out_specs=vmem,
        scratch_shapes=[
            pltpu.VMEM((head_count, half, lat_width), jnp.bfloat16),
            pltpu.VMEM((head_count, half, 128), jnp.float32),
            pltpu.VMEM((total_rows, out_proj.shape[0]), jnp.bfloat16),
            pltpu.VMEM((tensor_count, chunk, columns), jnp.bfloat16),
            pltpu.VMEM((tensor_count, chunk, columns), jnp.bfloat16),
            pltpu.VMEM((chunk, columns), jnp.float32),
            dma((1 + head_count,)),
            dma((1 + head_count,)),
            dma((pool_count,)),
            dma((pool_count,)),
            dma((pool_count,)),
            dma((pool_count,)),
            dma((tensor_count,)),
            dma((tensor_count,)),
            dma((tensor_count,)),
            dma((tensor_count,)),
        ],
        compiler_params=pltpu.CompilerParams(
            collective_id=0, has_side_effects=True, vmem_limit_bytes=40 * 1024 * 1024
        ),
        name="tail",
    )(o_parts, lse, value_absorb, out_proj)


PAGE_BATCH = 8
NEG = -1e30


def dot_keys(query, keys):
    return lax.dot_general(
        query, keys, (((1,), (1,)), ((), ())), preferred_element_type=jnp.float32
    )


def front_kernel(
    scale,
    page_row_ref,
    page_valid_ref,
    row_page_ref,
    pick_ref,
    states_ref,
    down_ref,
    gain_ref,
    cos_ref,
    sin_ref,
    query_ref,
    steps_ref,
    key_row_ref,
    key_step_ref,
    cache_ref,
    new_ref,
    o_ref,
    lse_ref,
    outgoing,
    incoming,
    summed_ref,
    finished,
    pool_out,
    arrived,
    pages,
    page_o,
    page_top,
    page_total,
    page_sem,
    sum_send,
    sum_recv,
    new_send,
    new_recv,
    pool_send,
    pool_recv,
    all_send,
    all_recv,
):
    tensor_count = lax.axis_size("tensor")
    pool_count = lax.axis_size("pool")
    depth = lax.axis_index("tensor")
    pool = lax.axis_index("pool")
    sub = states_ref.shape[2]
    width = down_ref.shape[1]
    lat_width = gain_ref.shape[1]
    row_count, per_row, _ = query_ref.shape
    page_len = cache_ref.shape[1]
    batches = row_count // PAGE_BATCH
    span = tensor_count // 2

    def page_copy(index):
        return pltpu.make_async_copy(
            cache_ref.at[pl.ds(index * PAGE_BATCH, PAGE_BATCH)],
            pages.at[lax.rem(index, 2)],
            page_sem.at[lax.rem(index, 2)],
        )

    page_copy(jnp.int32(0)).start()
    barrier = pltpu.get_barrier_semaphore()
    for step in range(1, tensor_count):
        pl.semaphore_signal(
            barrier,
            inc=1,
            device_id={"tensor": lax.rem(depth + step, tensor_count)},
            device_id_type=MESH,
        )
    for step in range(1, pool_count):
        pl.semaphore_signal(
            barrier,
            inc=1,
            device_id={"pool": lax.rem(pool + step, pool_count)},
            device_id_type=MESH,
        )
    pl.semaphore_wait(barrier, tensor_count + pool_count - 2)

    def partial(dest):
        rows = states_ref[:, dest].reshape(2 * sub, states_ref.shape[3])
        return jnp.dot(rows, down_ref[...], preferred_element_type=jnp.float32)

    def sum_copy(step):
        return pltpu.make_async_remote_copy(
            src_ref=outgoing.at[step],
            dst_ref=incoming.at[step],
            send_sem=sum_send.at[step],
            recv_sem=sum_recv.at[step],
            device_id={"tensor": lax.rem(depth + step, tensor_count)},
            device_id_type=MESH,
        )

    def all_copy(step):
        return pltpu.make_async_remote_copy(
            src_ref=arrived.at[depth],
            dst_ref=arrived.at[depth],
            send_sem=all_send.at[step],
            recv_sem=all_recv.at[step],
            device_id={"tensor": lax.rem(depth + step, tensor_count)},
            device_id_type=MESH,
        )

    def pool_copy(step):
        target = lax.rem(pool + step, pool_count)
        return pltpu.make_async_remote_copy(
            src_ref=pool_out.at[target],
            dst_ref=arrived.at[depth, pool],
            send_sem=pool_send.at[step],
            recv_sem=pool_recv.at[step],
            device_id={"pool": target},
            device_id_type=MESH,
        )

    def new_copy(block):
        return pltpu.make_async_remote_copy(
            src_ref=finished.at[block],
            dst_ref=new_ref.at[lax.rem(depth, 2)],
            send_sem=new_send.at[block],
            recv_sem=new_recv.at[lax.rem(depth, 2)],
            device_id={"tensor": block * span + depth // 2},
            device_id_type=MESH,
        )

    def each(first, last, body):
        def run(step, carry):
            body(step)
            return carry

        lax.fori_loop(first, last, run, 0)

    def send_partial(step):
        outgoing[step] = partial(lax.rem(depth + step, tensor_count)).astype(jnp.bfloat16)
        sum_copy(step).start()

    each(1, tensor_count, send_partial)
    summed_ref[...] = partial(depth)

    def attend_batch(index):
        @pl.when(index + 1 < batches)
        def _():
            page_copy(index + 1).start()

        page_copy(index).wait()
        slot = lax.rem(index, 2)
        for item in range(PAGE_BATCH):
            page = index * PAGE_BATCH + item
            query = query_ref[page_row_ref[page]]
            keys = pages[slot, item]
            scores = dot_keys(query, keys) * scale
            ids = lax.broadcasted_iota(jnp.int32, scores.shape, 1)
            valid = ids < page_valid_ref[page]
            scores = jnp.where(valid, scores, NEG)
            top = jnp.max(scores, axis=1, keepdims=True)
            weights = jnp.where(valid, jnp.exp(scores - top), 0.0)
            page_top[page] = jnp.broadcast_to(top, (per_row, 128))
            page_total[page] = jnp.broadcast_to(
                jnp.sum(weights, axis=1, keepdims=True), (per_row, 128)
            )
            page_o[page] = jnp.dot(
                weights.astype(jnp.bfloat16),
                keys[:, :lat_width],
                preferred_element_type=jnp.float32,
            )

    first_stop = batches // 2
    second_stop = first_stop + max(batches // 8, 1)
    each(0, first_stop, attend_batch)

    each(1, tensor_count, lambda step: sum_copy(step).wait_recv())

    def add_partial(step):
        summed_ref[...] += incoming[step].astype(jnp.float32)

    each(1, tensor_count, add_partial)
    latent = summed_ref[:, :lat_width]
    rotary = summed_ref[:, lat_width:]
    half_width = (width - lat_width) // 2
    normed = (
        latent
        * lax.rsqrt(jnp.mean(latent * latent, axis=1, keepdims=True) + EPSILON)
        * gain_ref[...]
    )
    swapped = jnp.concatenate([rotary[:, half_width:], rotary[:, :half_width]], axis=1)
    turned = rotary * cos_ref[...] + swapped * sin_ref[...]
    normed = normed.astype(jnp.bfloat16)
    turned = turned.astype(jnp.bfloat16)
    for block in range(2):
        finished[block, :, :lat_width] = normed[block * sub : (block + 1) * sub]
        finished[block, :, lat_width:] = turned[block * sub : (block + 1) * sub]

    def choose(target):
        first = pick_ref[0, target] > 0
        second = pick_ref[1, target] > 0
        none = jnp.zeros(finished.shape[1:], jnp.bfloat16)
        return jnp.where(first, finished[0], jnp.where(second, finished[1], none))

    def send_pool(step):
        target = lax.rem(pool + step, pool_count)
        pool_out[target] = choose(target)
        pool_copy(step).start()

    each(1, pool_count, send_pool)
    arrived[depth, pool] = choose(pool)
    for block in range(2):
        keep = block * span + depth // 2 == depth

        @pl.when(keep)
        def _(block=block):
            new_ref[lax.rem(depth, 2)] = finished[block]

    each(first_stop, second_stop, attend_batch)

    def pool_wait(step):
        pltpu.make_async_remote_copy(
            src_ref=pool_out.at[pool],
            dst_ref=arrived.at[depth, lax.rem(pool + pool_count - step, pool_count)],
            send_sem=pool_send.at[step],
            recv_sem=pool_recv.at[step],
            device_id={"pool": lax.rem(pool + step, pool_count)},
            device_id_type=MESH,
        ).wait_recv()

    each(1, pool_count, pool_wait)
    each(1, tensor_count, lambda step: all_copy(step).start())
    for block in range(2):

        @pl.when(block * span + depth // 2 != depth)
        def _(block=block):
            new_copy(block).start()

    each(second_stop, batches, attend_batch)

    def all_wait(step):
        source = lax.rem(depth + tensor_count - step, tensor_count)
        pltpu.make_async_remote_copy(
            src_ref=arrived.at[source],
            dst_ref=arrived.at[source],
            send_sem=all_send.at[step],
            recv_sem=all_recv.at[step],
            device_id={"tensor": source},
            device_id_type=MESH,
        ).wait_recv()

    each(1, tensor_count, all_wait)

    prompt_keys = tensor_count * pool_count * sub
    step_keys = steps_ref.shape[0]
    rows_in = 8
    lines = rows_in * per_row
    step_count = step_keys // row_count

    def merge(group):
        query = query_ref[pl.ds(group * rows_in, rows_in)].reshape(lines, width)
        line_ids = lax.broadcasted_iota(jnp.int32, (lines, 1), 0)
        row_ids = group * rows_in + line_ids // per_row
        step_ids = lax.rem(line_ids, step_count)
        top = []
        total = []
        mixed = []
        for item in range(rows_in):
            page = row_page_ref[group * rows_in + item]
            top.append(page_top[page])
            total.append(page_total[page])
            mixed.append(page_o[page])
        top = jnp.concatenate(top, axis=0)[:, :1]
        total = jnp.concatenate(total, axis=0)[:, :1]
        mixed = jnp.concatenate(mixed, axis=0)
        prompts = arrived[...].reshape(prompt_keys, width)
        own = steps_ref[...]

        def mask_of(first, count):
            keys_row = key_row_ref[:, first : first + count]
            keys_step = key_step_ref[:, first : first + count]
            return (keys_row == row_ids) & (keys_step <= step_ids)

        own_mask = mask_of(0, step_keys)
        new_mask = mask_of(step_keys, prompt_keys)
        own_scores = jnp.where(own_mask, dot_keys(query, own) * scale, NEG)
        new_scores = jnp.where(new_mask, dot_keys(query, prompts) * scale, NEG)
        best = jnp.maximum(
            top,
            jnp.maximum(
                jnp.max(own_scores, axis=1, keepdims=True),
                jnp.max(new_scores, axis=1, keepdims=True),
            ),
        )
        own_weights = jnp.where(own_mask, jnp.exp(own_scores - best), 0.0)
        new_weights = jnp.where(new_mask, jnp.exp(new_scores - best), 0.0)
        old = jnp.exp(top - best)
        total = (
            total * old
            + jnp.sum(own_weights, axis=1, keepdims=True)
            + jnp.sum(new_weights, axis=1, keepdims=True)
        )
        mixed = (
            mixed * old
            + jnp.dot(
                own_weights.astype(jnp.bfloat16),
                own[:, :lat_width],
                preferred_element_type=jnp.float32,
            )
            + jnp.dot(
                new_weights.astype(jnp.bfloat16),
                prompts[:, :lat_width],
                preferred_element_type=jnp.float32,
            )
        )
        positive = total > 0.0
        safe = jnp.where(positive, total, 1.0)
        place = pl.ds(pl.multiple_of(group * lines, lines), lines)
        o_ref[place, :] = (mixed / safe).astype(jnp.bfloat16)
        lse_ref[place, :] = jnp.broadcast_to(
            jnp.where(positive, best + jnp.log(safe), NEG), (lines, 128)
        )

    each(0, row_count // rows_in, merge)

    for slot in range(2):
        source = lax.rem(depth, span) * 2 + slot

        @pl.when(source != depth)
        def _(slot=slot, source=source):
            pltpu.make_async_remote_copy(
                src_ref=finished.at[0],
                dst_ref=new_ref.at[slot],
                send_sem=new_send.at[0],
                recv_sem=new_recv.at[slot],
                device_id={"tensor": source},
                device_id_type=MESH,
            ).wait_recv()

    for block in range(2):

        @pl.when(block * span + depth // 2 != depth)
        def _(block=block):
            new_copy(block).wait_send()

    each(1, tensor_count, lambda step: sum_copy(step).wait_send())
    each(1, tensor_count, lambda step: all_copy(step).wait_send())
    each(1, pool_count, lambda step: pool_copy(step).wait_send())


def front(scale, scalars, arrays, cache_pages):
    tensor_count = lax.axis_size("tensor")
    pool_count = lax.axis_size("pool")
    states, kv_down, kv_gain, _, _, queries = arrays[:6]
    sub = states.shape[2]
    width = kv_down.shape[1]
    lat_width = kv_gain.shape[1]
    row_count, per_row, _ = queries.shape
    lines = row_count * per_row
    vmem = pl.BlockSpec(memory_space=pltpu.VMEM)
    dma = pltpu.SemaphoreType.DMA
    return pl.pallas_call(
        functools.partial(front_kernel, scale),
        out_shape=(
            jax.ShapeDtypeStruct((2, sub, width), jnp.bfloat16),
            jax.ShapeDtypeStruct((lines, lat_width), jnp.bfloat16),
            jax.ShapeDtypeStruct((lines, 128), jnp.float32),
        ),
        in_specs=[pl.BlockSpec(memory_space=pltpu.SMEM)] * len(scalars)
        + [vmem] * len(arrays)
        + [pl.BlockSpec(memory_space=pl.ANY)],
        out_specs=(vmem, vmem, vmem),
        scratch_shapes=[
            pltpu.VMEM((tensor_count, 2 * sub, width), jnp.bfloat16),
            pltpu.VMEM((tensor_count, 2 * sub, width), jnp.bfloat16),
            pltpu.VMEM((2 * sub, width), jnp.float32),
            pltpu.VMEM((2, sub, width), jnp.bfloat16),
            pltpu.VMEM((pool_count, sub, width), jnp.bfloat16),
            pltpu.VMEM((tensor_count, pool_count, sub, width), jnp.bfloat16),
            pltpu.VMEM((2, PAGE_BATCH) + cache_pages.shape[1:], jnp.bfloat16),
            pltpu.VMEM((row_count, per_row, lat_width), jnp.float32),
            pltpu.VMEM((row_count, per_row, 128), jnp.float32),
            pltpu.VMEM((row_count, per_row, 128), jnp.float32),
            dma((2,)),
            dma((tensor_count,)),
            dma((tensor_count,)),
            dma((2,)),
            dma((2,)),
            dma((pool_count,)),
            dma((pool_count,)),
            dma((tensor_count,)),
            dma((tensor_count,)),
        ],
        compiler_params=pltpu.CompilerParams(
            collective_id=1, has_side_effects=True, vmem_limit_bytes=48 * 1024 * 1024
        ),
        name="front",
    )(*scalars, *arrays, cache_pages)


def local(
    prompt_states,
    kv_down,
    kv_gain,
    queries,
    step_latents,
    key_absorb,
    value_absorb,
    out_proj,
    cache_pages,
    page_table,
    cache_len,
    owner_map,
    senders,
    prompt_lens,
):
    tensor_count = lax.axis_size("tensor")
    pool_count = lax.axis_size("pool")
    seq_count = lax.axis_size("seq")
    pool_index = lax.axis_index("pool")
    seq_index = lax.axis_index("seq")
    tensor_index = lax.axis_index("tensor")
    pre_rows = prompt_states.shape[1]
    half_rows = pre_rows // 2
    sub = half_rows // tensor_count
    row_count = queries.shape[0]
    lat_width = kv_gain.shape[0]
    width = kv_down.shape[1]
    head_count = key_absorb.shape[0]
    nope_width = key_absorb.shape[1]
    step_count = queries.shape[1]
    query_width = queries.shape[2] // head_count
    page_len = cache_pages.shape[1]
    group_index = pool_index * seq_count + seq_index

    piece_ids = jnp.arange(2 * sub, dtype=jnp.int32)
    row_ids = (
        group_index * pre_rows
        + piece_ids // sub * half_rows
        + tensor_index * sub
        + piece_ids % sub
    )
    _, positions = rows_meta(row_ids, owner_map, senders, cache_len, half_rows)
    half_width = (width - lat_width) // 2
    inv_freq = THETA ** (-(jnp.arange(half_width, dtype=jnp.float32) * 2.0 / (2 * half_width)))
    angles = positions.astype(jnp.float32)[:, None] * inv_freq[None, :]
    cosine = jnp.cos(angles)
    sine = jnp.sin(angles)
    cos_full = jnp.concatenate([cosine, cosine], axis=1)
    sin_full = jnp.concatenate([-sine, sine], axis=1)

    pool_ids = jnp.arange(pool_count, dtype=jnp.int32)
    pairs = 2 * (pool_ids * seq_count + seq_index)[:, None] + jnp.arange(2, dtype=jnp.int32)
    flat_pairs = pairs.reshape(-1)
    targets = lookup(lookup(flat_pairs, senders), owner_map).reshape(pool_count, 2)
    lengths = lookup(flat_pairs, prompt_lens).reshape(pool_count, 2)
    mine = targets // row_count == pool_index
    target_rows = targets % row_count
    label = jnp.where(mine[:, 0], target_rows[:, 0], jnp.where(mine[:, 1], target_rows[:, 1], -1))
    length = jnp.where(mine[:, 0], lengths[:, 0], jnp.where(mine[:, 1], lengths[:, 1], 0))
    own_targets = lookup(
        lookup(2 * group_index + jnp.arange(2, dtype=jnp.int32), senders), owner_map
    )
    pick = (own_targets[:, None] // row_count == pool_ids[None, :]).astype(jnp.int32)

    page_ids = page_table[:, 0, 0]
    local_rows = jnp.arange(row_count, dtype=jnp.int32)
    matches = (page_ids[None, :] == local_rows[:, None]).astype(jnp.int32)
    local_len = lax.dynamic_slice_in_dim(cache_len, pool_index * row_count, row_count, 0)
    page_rows = jnp.sum(matches * local_rows[None, :], axis=1)
    page_valid = jnp.clip(
        jnp.sum(matches * local_len[None, :], axis=1) - seq_index * page_len, 0, page_len
    )
    slot_ids = (
        jnp.arange(tensor_count, dtype=jnp.int32)[:, None, None] * sub
        + jnp.arange(sub, dtype=jnp.int32)[None, None, :]
    )
    prompt_row = jnp.where(slot_ids < length[None, :, None], label[None, :, None], -1).reshape(-1)
    step_row = jnp.where(seq_index == 0, jnp.repeat(local_rows, step_count), -1)
    key_row = jnp.concatenate([step_row, prompt_row])[None, :]
    key_step = jnp.concatenate(
        [
            jnp.tile(jnp.arange(step_count, dtype=jnp.int32), row_count),
            jnp.zeros_like(prompt_row),
        ]
    )[None, :]

    query_heads = queries.reshape(row_count, step_count, head_count, query_width)
    q_lat = jnp.einsum(
        "rshn,hnl->rhsl",
        query_heads[..., :nope_width],
        key_absorb,
        preferred_element_type=jnp.float32,
    ).astype(jnp.bfloat16)
    query_cat = jnp.concatenate(
        [q_lat, query_heads[..., nope_width:].transpose(0, 2, 1, 3)], axis=3
    ).reshape(row_count, head_count * step_count, width)
    new_pieces, o_lines, lse_lines = front(
        float(query_width) ** (-0.5),
        (page_rows, page_valid, page_ids, pick),
        (
            prompt_states.reshape(2, tensor_count, sub, prompt_states.shape[2]),
            kv_down,
            kv_gain[None, :],
            cos_full,
            sin_full,
            query_cat,
            step_latents.reshape(row_count * step_count, width),
            key_row,
            key_step,
        ),
        cache_pages,
    )
    new_latents = new_pieces.reshape(1, 2 * sub, width)
    half = row_count * step_count // 2

    def by_head(lines):
        split = lines.reshape(2, row_count // 2, head_count, step_count, lines.shape[1])
        return split.transpose(0, 2, 1, 3, 4).reshape(2, head_count, half, lines.shape[1])

    attended = tail(by_head(o_lines), by_head(lse_lines), value_absorb, out_proj).reshape(
        -1, step_count, out_proj.shape[1]
    )
    return (new_latents, attended)


def solution(mesh):
    placed = (
        P(("groups", "pool", "seq"), None, "tensor"),
        P("tensor", None),
        P(),
        P(("groups", "pool"), None, "tensor"),
        P(("groups", "pool"), None, None),
        P("tensor", None, None),
        P("tensor", None, None),
        P("tensor", ("pool", "seq")),
        P(("groups", "pool", "seq"), None, None),
        P(("groups", "pool"), "seq", None),
        P("groups"),
        P("groups"),
        P("groups"),
        P("groups"),
    )
    return jax.shard_map(
        local,
        mesh=mesh,
        in_specs=placed,
        out_specs=(
            P(("groups", "pool", "seq"), "tensor", None),
            P(("groups", "tensor"), None, ("pool", "seq")),
        ),
        check_vma=False,
    )
```

```python
import functools

import jax
import jax.numpy as jnp
from jax import lax
from jax.experimental import pallas as pl
from jax.experimental.pallas import tpu as pltpu
from jax.sharding import PartitionSpec as P

EPSILON = 1e-06
THETA = 10000.0


MESH = pl.DeviceIdType.MESH


def tail_kernel(
    o_ref,
    lse_ref,
    absorb_ref,
    proj_ref,
    out_ref,
    o_in,
    lse_in,
    heads,
    up,
    down,
    total_ref,
    pair_send,
    pair_recv,
    gather_send,
    gather_recv,
    forward_send,
    forward_recv,
    up_send,
    up_recv,
    down_send,
    down_recv,
):
    tensor_count = lax.axis_size("tensor")
    pool_count = lax.axis_size("pool")
    depth = lax.axis_index("tensor")
    pool = lax.axis_index("pool")
    seq = lax.axis_index("seq")
    head_count, half, _ = o_ref.shape[1:]
    value_width = absorb_ref.shape[2]
    chunk = out_ref.shape[0]
    other = 1 - seq
    has_below = depth > 0
    has_above = depth < tensor_count - 1

    barrier = pltpu.get_barrier_semaphore()
    pl.semaphore_signal(barrier, inc=1, device_id={"seq": other}, device_id_type=MESH)
    for step in range(1, pool_count):
        pl.semaphore_signal(
            barrier,
            inc=1,
            device_id={"pool": lax.rem(pool + step, pool_count)},
            device_id_type=MESH,
        )

    @pl.when(has_below)
    def _():
        pl.semaphore_signal(barrier, inc=1, device_id={"tensor": depth - 1}, device_id_type=MESH)

    @pl.when(has_above)
    def _():
        pl.semaphore_signal(barrier, inc=1, device_id={"tensor": depth + 1}, device_id_type=MESH)

    pl.semaphore_wait(
        barrier, pool_count + has_below.astype(jnp.int32) + has_above.astype(jnp.int32)
    )

    pair = [
        pltpu.make_async_remote_copy(
            src_ref=lse_ref.at[other],
            dst_ref=lse_in,
            send_sem=pair_send.at[0],
            recv_sem=pair_recv.at[0],
            device_id={"seq": other},
            device_id_type=MESH,
        )
    ] + [
        pltpu.make_async_remote_copy(
            src_ref=o_ref.at[other, h],
            dst_ref=o_in.at[h],
            send_sem=pair_send.at[1 + h],
            recv_sem=pair_recv.at[1 + h],
            device_id={"seq": other},
            device_id_type=MESH,
        )
        for h in range(head_count)
    ]
    for copy in pair:
        copy.start()
    own_rows = pl.ds(pl.multiple_of((pool * 2 + seq) * half, half), half)
    pair[0].wait_recv()
    for h in range(head_count):
        pair[1 + h].wait_recv()
        mine = lse_ref[seq, h][:, :1]
        theirs = lse_in[h][:, :1]
        ratio = 1.0 / (1.0 + jnp.exp(jnp.clip(theirs - mine, -80.0, 80.0)))
        merged = o_ref[seq, h].astype(jnp.float32) * ratio + o_in[h].astype(jnp.float32) * (
            1.0 - ratio
        )
        heads[own_rows, h * value_width : (h + 1) * value_width] = jnp.dot(
            merged.astype(jnp.bfloat16), absorb_ref[h], preferred_element_type=jnp.float32
        ).astype(jnp.bfloat16)

    def rows_of(pool_id, seq_id):
        return pl.ds(pl.multiple_of((pool_id * 2 + seq_id) * half, half), half)

    gathers = []
    for step in range(1, pool_count):
        gathers.append(
            pltpu.make_async_remote_copy(
                src_ref=heads.at[own_rows],
                dst_ref=heads.at[own_rows],
                send_sem=gather_send.at[step],
                recv_sem=gather_recv.at[step],
                device_id={"pool": lax.rem(pool + step, pool_count)},
                device_id_type=MESH,
            )
        )
    forwards = []
    for step in range(pool_count):
        rows = rows_of(lax.rem(pool + pool_count - step, pool_count), seq)
        forwards.append(
            pltpu.make_async_remote_copy(
                src_ref=heads.at[rows],
                dst_ref=heads.at[rows],
                send_sem=forward_send.at[step],
                recv_sem=forward_recv.at[step],
                device_id={"seq": other},
                device_id_type=MESH,
            )
        )
    for copy in gathers:
        copy.start()
    forwards[0].start()
    for step in range(1, pool_count):
        gathers[step - 1].wait_recv()
        forwards[step].start()
    for copy in forwards:
        copy.wait_recv()

    def project(dest):
        rows = pl.ds(pl.multiple_of(dest * chunk, chunk), chunk)
        return jnp.dot(heads[rows, :], proj_ref[...], preferred_element_type=jnp.float32)

    def lane_copy(buffer, send, recv, dest, target):
        return pltpu.make_async_remote_copy(
            src_ref=buffer.at[dest],
            dst_ref=buffer.at[dest],
            send_sem=send.at[dest],
            recv_sem=recv.at[dest],
            device_id={"tensor": target},
            device_id_type=MESH,
        )

    def pass_on(buffer, send, recv, dest, target, has_source):
        part = project(dest)
        copy = lane_copy(buffer, send, recv, dest, target)

        @pl.when(has_source)
        def _():
            copy.wait_recv()
            buffer[dest] = (buffer[dest].astype(jnp.float32) + part).astype(jnp.bfloat16)

        @pl.when(jnp.logical_not(has_source))
        def _():
            buffer[dest] = part.astype(jnp.bfloat16)

        copy.start()

    def turn(step, carry):
        high = tensor_count - 1 - step

        @pl.when(high > depth)
        def _():
            pass_on(up, up_send, up_recv, high, depth + 1, has_below)

        @pl.when(step < depth)
        def _():
            pass_on(down, down_send, down_recv, step, depth - 1, has_above)

        return carry

    lax.fori_loop(0, tensor_count - 1, turn, 0)
    total = project(depth)

    total_ref[...] = total

    @pl.when(has_below)
    def _():
        lane_copy(up, up_send, up_recv, depth, depth - 1).wait_recv()
        total_ref[...] += up[depth].astype(jnp.float32)

    @pl.when(has_above)
    def _():
        lane_copy(down, down_send, down_recv, depth, depth + 1).wait_recv()
        total_ref[...] += down[depth].astype(jnp.float32)

    out_ref[...] = total_ref[...].astype(jnp.bfloat16)

    def drain(step, carry):
        high = tensor_count - 1 - step

        @pl.when(high > depth)
        def _():
            lane_copy(up, up_send, up_recv, high, depth + 1).wait_send()

        @pl.when(step < depth)
        def _():
            lane_copy(down, down_send, down_recv, step, depth - 1).wait_send()

        return carry

    lax.fori_loop(0, tensor_count - 1, drain, 0)
    for copy in pair + gathers + forwards:
        copy.wait_send()


def tail(o_parts, lse, value_absorb, out_proj):
    tensor_count = lax.axis_size("tensor")
    pool_count = lax.axis_size("pool")
    _, head_count, half, lat_width = o_parts.shape
    columns = out_proj.shape[1]
    total_rows = pool_count * 2 * half
    chunk = total_rows // tensor_count
    vmem = pl.BlockSpec(memory_space=pltpu.VMEM)
    dma = pltpu.SemaphoreType.DMA
    return pl.pallas_call(
        tail_kernel,
        out_shape=jax.ShapeDtypeStruct((chunk, columns), jnp.bfloat16),
        in_specs=[vmem] * 4,
        out_specs=vmem,
        scratch_shapes=[
            pltpu.VMEM((head_count, half, lat_width), jnp.bfloat16),
            pltpu.VMEM((head_count, half, 128), jnp.float32),
            pltpu.VMEM((total_rows, out_proj.shape[0]), jnp.bfloat16),
            pltpu.VMEM((tensor_count, chunk, columns), jnp.bfloat16),
            pltpu.VMEM((tensor_count, chunk, columns), jnp.bfloat16),
            pltpu.VMEM((chunk, columns), jnp.float32),
            dma((1 + head_count,)),
            dma((1 + head_count,)),
            dma((pool_count,)),
            dma((pool_count,)),
            dma((pool_count,)),
            dma((pool_count,)),
            dma((tensor_count,)),
            dma((tensor_count,)),
            dma((tensor_count,)),
            dma((tensor_count,)),
        ],
        compiler_params=pltpu.CompilerParams(
            collective_id=0, has_side_effects=True, vmem_limit_bytes=40 * 1024 * 1024
        ),
        name="tail",
    )(o_parts, lse, value_absorb, out_proj)


PAGE_BATCH = 8
NEG = -1e30


def dot_keys(query, keys):
    return lax.dot_general(
        query, keys, (((1,), (1,)), ((), ())), preferred_element_type=jnp.float32
    )


def front_kernel(
    scale,
    page_row_ref,
    row_page_ref,
    cache_len_ref,
    owner_ref,
    senders_ref,
    prompt_lens_ref,
    states_ref,
    down_ref,
    gain_ref,
    freq_ref,
    query_ref,
    steps_ref,
    cache_ref,
    new_ref,
    o_ref,
    lse_ref,
    outgoing,
    incoming,
    summed_ref,
    finished,
    pool_out,
    arrived,
    pages,
    page_o,
    page_top,
    page_total,
    page_sem,
    sum_send,
    sum_recv,
    new_send,
    new_recv,
    pool_send,
    pool_recv,
    all_send,
    all_recv,
):
    tensor_count = lax.axis_size("tensor")
    pool_count = lax.axis_size("pool")
    depth = lax.axis_index("tensor")
    pool = lax.axis_index("pool")
    sub = states_ref.shape[2]
    width = down_ref.shape[0]
    lat_width = gain_ref.shape[1]
    row_count, per_row, _ = query_ref.shape
    page_len = cache_ref.shape[2]
    seq = lax.axis_index("seq")
    seq_count = lax.axis_size("seq")
    batches = row_count // PAGE_BATCH
    span = tensor_count // 2

    def page_copy(index):
        return pltpu.make_async_copy(
            cache_ref.at[pl.ds(index * PAGE_BATCH, PAGE_BATCH)],
            pages.at[lax.rem(index, 2)],
            page_sem.at[lax.rem(index, 2)],
        )

    page_copy(jnp.int32(0)).start()
    barrier = pltpu.get_barrier_semaphore()
    for step in range(1, tensor_count):
        pl.semaphore_signal(
            barrier,
            inc=1,
            device_id={"tensor": lax.rem(depth + step, tensor_count)},
            device_id_type=MESH,
        )
    for step in range(1, pool_count):
        pl.semaphore_signal(
            barrier,
            inc=1,
            device_id={"pool": lax.rem(pool + step, pool_count)},
            device_id_type=MESH,
        )
    pl.semaphore_wait(barrier, tensor_count + pool_count - 2)

    def partial(dest):
        rows = states_ref[:, dest].reshape(2 * sub, states_ref.shape[3])
        return dot_keys(rows, down_ref[...])

    def sum_copy(step):
        return pltpu.make_async_remote_copy(
            src_ref=outgoing.at[step],
            dst_ref=incoming.at[step],
            send_sem=sum_send.at[step],
            recv_sem=sum_recv.at[step],
            device_id={"tensor": lax.rem(depth + step, tensor_count)},
            device_id_type=MESH,
        )

    def all_copy(step):
        return pltpu.make_async_remote_copy(
            src_ref=arrived.at[depth],
            dst_ref=arrived.at[depth],
            send_sem=all_send.at[step],
            recv_sem=all_recv.at[step],
            device_id={"tensor": lax.rem(depth + step, tensor_count)},
            device_id_type=MESH,
        )

    def pool_copy(step):
        target = lax.rem(pool + step, pool_count)
        return pltpu.make_async_remote_copy(
            src_ref=pool_out.at[target],
            dst_ref=arrived.at[depth, pool],
            send_sem=pool_send.at[step],
            recv_sem=pool_recv.at[step],
            device_id={"pool": target},
            device_id_type=MESH,
        )

    def new_copy(block):
        return pltpu.make_async_remote_copy(
            src_ref=finished.at[block],
            dst_ref=new_ref.at[lax.rem(depth, 2)],
            send_sem=new_send.at[block],
            recv_sem=new_recv.at[lax.rem(depth, 2)],
            device_id={"tensor": block * span + depth // 2},
            device_id_type=MESH,
        )

    def each(first, last, body):
        def run(step, carry):
            body(step)
            return carry

        lax.fori_loop(first, last, run, 0)

    def send_partial(step):
        outgoing[step] = partial(lax.rem(depth + step, tensor_count)).astype(jnp.bfloat16)
        sum_copy(step).start()

    each(1, tensor_count, send_partial)
    summed_ref[...] = partial(depth)

    def attend_batch(index):
        @pl.when(index + 1 < batches)
        def _():
            page_copy(index + 1).start()

        page_copy(index).wait()
        slot = lax.rem(index, 2)
        for item in range(PAGE_BATCH):
            page = index * PAGE_BATCH + item
            row = page_row_ref[page]
            query = query_ref[row]
            keys = pages[slot, item]
            scores = jnp.dot(query, keys, preferred_element_type=jnp.float32) * scale
            ids = lax.broadcasted_iota(jnp.int32, scores.shape, 1)
            valid = ids < cache_len_ref[pool * row_count + row] - seq * page_len
            scores = jnp.where(valid, scores, NEG)
            top = jnp.max(scores, axis=1, keepdims=True)
            weights = jnp.where(valid, jnp.exp(scores - top), 0.0)
            page_top[page] = jnp.broadcast_to(top, (per_row, 128))
            page_total[page] = jnp.broadcast_to(
                jnp.sum(weights, axis=1, keepdims=True), (per_row, 128)
            )
            page_o[page] = dot_keys(weights.astype(jnp.bfloat16), keys[:lat_width])

    first_stop = batches // 2
    second_stop = first_stop + max(batches // 8, 1)
    each(0, first_stop, attend_batch)

    each(1, tensor_count, lambda step: sum_copy(step).wait_recv())

    def add_partial(step):
        summed_ref[...] += incoming[step].astype(jnp.float32)

    each(1, tensor_count, add_partial)
    latent = summed_ref[:, :lat_width]
    rotary = summed_ref[:, lat_width:]
    half_width = (width - lat_width) // 2
    normed = (
        latent
        * lax.rsqrt(jnp.mean(latent * latent, axis=1, keepdims=True) + EPSILON)
        * gain_ref[...]
    )
    swapped = jnp.concatenate([rotary[:, half_width:], rotary[:, :half_width]], axis=1)
    line_ids = lax.broadcasted_iota(jnp.int32, (2 * sub, 1), 0)
    own_first = 2 * (pool * seq_count + seq)
    own_rows = [owner_ref[senders_ref[own_first + block]] for block in range(2)]
    bases = [cache_len_ref[row] for row in own_rows]
    positions = jnp.where(line_ids < sub, bases[0], bases[1]) + depth * sub + lax.rem(line_ids, sub)
    angles = positions.astype(jnp.float32) * freq_ref[...]
    lanes = lax.broadcasted_iota(jnp.int32, (1, 2 * half_width), 1)
    sine = jnp.where(lanes < half_width, -1.0, 1.0) * jnp.sin(angles)
    turned = rotary * jnp.cos(angles) + swapped * sine
    normed = normed.astype(jnp.bfloat16)
    turned = turned.astype(jnp.bfloat16)
    for block in range(2):
        finished[block, :, :lat_width] = normed[block * sub : (block + 1) * sub]
        finished[block, :, lat_width:] = turned[block * sub : (block + 1) * sub]

    def choose(target):
        first = own_rows[0] // row_count == target
        second = own_rows[1] // row_count == target
        none = jnp.zeros(finished.shape[1:], jnp.bfloat16)
        return jnp.where(first, finished[0], jnp.where(second, finished[1], none))

    def send_pool(step):
        target = lax.rem(pool + step, pool_count)
        pool_out[target] = choose(target)
        pool_copy(step).start()

    each(1, pool_count, send_pool)
    arrived[depth, pool] = choose(pool)
    for block in range(2):
        keep = block * span + depth // 2 == depth

        @pl.when(keep)
        def _(block=block):
            new_ref[lax.rem(depth, 2)] = finished[block]

    each(first_stop, second_stop, attend_batch)

    def pool_wait(step):
        pltpu.make_async_remote_copy(
            src_ref=pool_out.at[pool],
            dst_ref=arrived.at[depth, lax.rem(pool + pool_count - step, pool_count)],
            send_sem=pool_send.at[step],
            recv_sem=pool_recv.at[step],
            device_id={"pool": lax.rem(pool + step, pool_count)},
            device_id_type=MESH,
        ).wait_recv()

    each(1, pool_count, pool_wait)
    each(1, tensor_count, lambda step: all_copy(step).start())
    for block in range(2):

        @pl.when(block * span + depth // 2 != depth)
        def _(block=block):
            new_copy(block).start()

    each(second_stop, batches, attend_batch)

    def all_wait(step):
        source = lax.rem(depth + tensor_count - step, tensor_count)
        pltpu.make_async_remote_copy(
            src_ref=arrived.at[source],
            dst_ref=arrived.at[source],
            send_sem=all_send.at[step],
            recv_sem=all_recv.at[step],
            device_id={"tensor": source},
            device_id_type=MESH,
        ).wait_recv()

    each(1, tensor_count, all_wait)

    prompt_keys = tensor_count * pool_count * sub
    step_keys = steps_ref.shape[0]
    rows_in = 8
    lines = rows_in * per_row
    step_count = step_keys // row_count
    head_count = per_row // step_count
    groups = row_count // rows_in
    key_ids = lax.broadcasted_iota(jnp.int32, (1, prompt_keys), 1)
    key_pool = lax.rem(key_ids // sub, pool_count)
    key_slot = key_ids // (pool_count * sub) * sub + lax.rem(key_ids, sub)
    new_row = jnp.full((1, prompt_keys), -1, jnp.int32)
    for source in range(pool_count):
        for block in range(2):
            sender = 2 * (source * seq_count + seq) + block
            target = owner_ref[senders_ref[sender]]
            local_row = target - pool * row_count
            local_row = jnp.where((local_row >= 0) & (local_row < row_count), local_row, -1)
            hit = (key_pool == source) & (key_slot < prompt_lens_ref[sender]) & (local_row >= 0)
            new_row = jnp.where(hit, local_row, new_row)
    own_ids = lax.broadcasted_iota(jnp.int32, (1, step_keys), 1)
    own_row = jnp.where(seq == 0, own_ids // step_count, -1)
    own_step = lax.rem(own_ids, step_count)
    to_lines = lax.broadcasted_iota(jnp.int32, (lines, lines), 0)
    from_lines = lax.broadcasted_iota(jnp.int32, (lines, lines), 1)
    per_head = rows_in * step_count
    source_line = (
        lax.rem(to_lines // step_count, rows_in) * per_row
        + to_lines // per_head * step_count
        + lax.rem(to_lines, step_count)
    )
    permutation = (from_lines == source_line).astype(jnp.float32)

    def merge(group):
        query = query_ref[pl.ds(group * rows_in, rows_in)].reshape(lines, width)
        line_ids = lax.broadcasted_iota(jnp.int32, (lines, 1), 0)
        row_ids = group * rows_in + line_ids // per_row
        step_ids = lax.rem(line_ids, step_count)
        top = []
        total = []
        mixed = []
        for item in range(rows_in):
            page = row_page_ref[group * rows_in + item]
            top.append(page_top[page])
            total.append(page_total[page])
            mixed.append(page_o[page])
        top = jnp.concatenate(top, axis=0)[:, :1]
        total = jnp.concatenate(total, axis=0)[:, :1]
        mixed = jnp.concatenate(mixed, axis=0)
        prompts = arrived[...].reshape(prompt_keys, width)
        own = steps_ref[...]

        own_mask = (own_row == row_ids) & (own_step <= step_ids)
        new_mask = new_row == row_ids
        own_scores = jnp.where(own_mask, dot_keys(query, own) * scale, NEG)
        new_scores = jnp.where(new_mask, dot_keys(query, prompts) * scale, NEG)
        best = jnp.maximum(
            top,
            jnp.maximum(
                jnp.max(own_scores, axis=1, keepdims=True),
                jnp.max(new_scores, axis=1, keepdims=True),
            ),
        )
        own_weights = jnp.where(own_mask, jnp.exp(own_scores - best), 0.0)
        new_weights = jnp.where(new_mask, jnp.exp(new_scores - best), 0.0)
        old = jnp.exp(top - best)
        total = (
            total * old
            + jnp.sum(own_weights, axis=1, keepdims=True)
            + jnp.sum(new_weights, axis=1, keepdims=True)
        )
        mixed = (
            mixed * old
            + jnp.dot(
                own_weights.astype(jnp.bfloat16),
                own[:, :lat_width],
                preferred_element_type=jnp.float32,
            )
            + jnp.dot(
                new_weights.astype(jnp.bfloat16),
                prompts[:, :lat_width],
                preferred_element_type=jnp.float32,
            )
        )
        positive = total > 0.0
        safe = jnp.where(positive, total, 1.0)
        by_head = jnp.dot(
            permutation.astype(jnp.bfloat16),
            (mixed / safe).astype(jnp.bfloat16),
            preferred_element_type=jnp.float32,
        ).astype(jnp.bfloat16)
        lse = jnp.broadcast_to(jnp.where(positive, best + jnp.log(safe), NEG), (lines, 128))
        lse_by_head = jnp.dot(
            permutation, lse, precision=lax.Precision.HIGHEST, preferred_element_type=jnp.float32
        )
        part = group // (groups // 2)
        start = pl.multiple_of(lax.rem(group, groups // 2) * per_head, per_head)
        for head in range(head_count):
            taken = slice(head * per_head, (head + 1) * per_head)
            o_ref[part, head, pl.ds(start, per_head), :] = by_head[taken]
            lse_ref[part, head, pl.ds(start, per_head), :] = lse_by_head[taken]

    each(0, row_count // rows_in, merge)

    for slot in range(2):
        source = lax.rem(depth, span) * 2 + slot

        @pl.when(source != depth)
        def _(slot=slot, source=source):
            pltpu.make_async_remote_copy(
                src_ref=finished.at[0],
                dst_ref=new_ref.at[slot],
                send_sem=new_send.at[0],
                recv_sem=new_recv.at[slot],
                device_id={"tensor": source},
                device_id_type=MESH,
            ).wait_recv()

    for block in range(2):

        @pl.when(block * span + depth // 2 != depth)
        def _(block=block):
            new_copy(block).wait_send()

    each(1, tensor_count, lambda step: sum_copy(step).wait_send())
    each(1, tensor_count, lambda step: all_copy(step).wait_send())
    each(1, pool_count, lambda step: pool_copy(step).wait_send())


def front(scale, scalars, arrays, cache_pages):
    tensor_count = lax.axis_size("tensor")
    pool_count = lax.axis_size("pool")
    states, kv_down, kv_gain, _, queries, steps = arrays
    sub = states.shape[2]
    width = kv_down.shape[0]
    lat_width = kv_gain.shape[1]
    row_count, per_row, _ = queries.shape
    step_count = steps.shape[0] // row_count
    heads_shape = (2, per_row // step_count, row_count * step_count // 2)
    vmem = pl.BlockSpec(memory_space=pltpu.VMEM)
    dma = pltpu.SemaphoreType.DMA
    return pl.pallas_call(
        functools.partial(front_kernel, scale),
        out_shape=(
            jax.ShapeDtypeStruct((2, sub, width), jnp.bfloat16),
            jax.ShapeDtypeStruct((*heads_shape, lat_width), jnp.bfloat16),
            jax.ShapeDtypeStruct((*heads_shape, 128), jnp.float32),
        ),
        in_specs=[pl.BlockSpec(memory_space=pltpu.SMEM)] * len(scalars)
        + [vmem] * len(arrays)
        + [pl.BlockSpec(memory_space=pl.ANY)],
        out_specs=(vmem, vmem, vmem),
        scratch_shapes=[
            pltpu.VMEM((tensor_count, 2 * sub, width), jnp.bfloat16),
            pltpu.VMEM((tensor_count, 2 * sub, width), jnp.bfloat16),
            pltpu.VMEM((2 * sub, width), jnp.float32),
            pltpu.VMEM((2, sub, width), jnp.bfloat16),
            pltpu.VMEM((pool_count, sub, width), jnp.bfloat16),
            pltpu.VMEM((tensor_count, pool_count, sub, width), jnp.bfloat16),
            pltpu.VMEM((2, PAGE_BATCH) + cache_pages.shape[1:], jnp.bfloat16),
            pltpu.VMEM((row_count, per_row, lat_width), jnp.float32),
            pltpu.VMEM((row_count, per_row, 128), jnp.float32),
            pltpu.VMEM((row_count, per_row, 128), jnp.float32),
            dma((2,)),
            dma((tensor_count,)),
            dma((tensor_count,)),
            dma((2,)),
            dma((2,)),
            dma((pool_count,)),
            dma((pool_count,)),
            dma((tensor_count,)),
            dma((tensor_count,)),
        ],
        compiler_params=pltpu.CompilerParams(
            collective_id=1, has_side_effects=True, vmem_limit_bytes=48 * 1024 * 1024
        ),
        name="front",
    )(*scalars, *arrays, cache_pages)


def local(
    prompt_states,
    kv_down,
    kv_gain,
    queries,
    step_latents,
    key_absorb,
    value_absorb,
    out_proj,
    cache_pages,
    page_table,
    cache_len,
    owner_map,
    senders,
    prompt_lens,
):
    tensor_count = lax.axis_size("tensor")
    sub = prompt_states.shape[1] // 2 // tensor_count
    row_count = queries.shape[0]
    lat_width = kv_gain.shape[0]
    width = kv_down.shape[1]
    head_count = key_absorb.shape[0]
    nope_width = key_absorb.shape[1]
    step_count = queries.shape[1]
    query_width = queries.shape[2] // head_count
    half_width = (width - lat_width) // 2
    inv_freq = THETA ** (-(jnp.arange(half_width, dtype=jnp.float32) * 2.0 / (2 * half_width)))
    page_ids = page_table[:, 0, 0]
    local_rows = jnp.arange(row_count, dtype=jnp.int32)
    matches = (page_ids[None, :] == local_rows[:, None]).astype(jnp.int32)
    page_rows = jnp.sum(matches * local_rows[None, :], axis=1)
    query_heads = queries.reshape(row_count, step_count, head_count, query_width)
    q_lat = jnp.einsum(
        "rshn,hnl->rhsl",
        query_heads[..., :nope_width],
        key_absorb,
        preferred_element_type=jnp.float32,
    ).astype(jnp.bfloat16)
    query_cat = jnp.concatenate(
        [q_lat, query_heads[..., nope_width:].transpose(0, 2, 1, 3)], axis=3
    ).reshape(row_count, head_count * step_count, width)
    new_pieces, o_parts, lse_parts = front(
        float(query_width) ** (-0.5),
        (page_rows, page_ids, cache_len, owner_map, senders, prompt_lens),
        (
            prompt_states.reshape(2, tensor_count, sub, prompt_states.shape[2]),
            kv_down.T,
            kv_gain[None, :],
            jnp.concatenate([inv_freq, inv_freq])[None, :],
            query_cat,
            step_latents.reshape(row_count * step_count, width),
        ),
        cache_pages.transpose(0, 2, 1),
    )
    new_latents = new_pieces.reshape(1, 2 * sub, width)
    attended = tail(o_parts, lse_parts, value_absorb, out_proj).reshape(
        -1, step_count, out_proj.shape[1]
    )
    return (new_latents, attended)


def solution(mesh):
    placed = (
        P(("groups", "pool", "seq"), None, "tensor"),
        P("tensor", None),
        P(),
        P(("groups", "pool"), None, "tensor"),
        P(("groups", "pool"), None, None),
        P("tensor", None, None),
        P("tensor", None, None),
        P("tensor", ("pool", "seq")),
        P(("groups", "pool", "seq"), None, None),
        P(("groups", "pool"), "seq", None),
        P("groups"),
        P("groups"),
        P("groups"),
        P("groups"),
    )
    return jax.shard_map(
        local,
        mesh=mesh,
        in_specs=placed,
        out_specs=(
            P(("groups", "pool", "seq"), "tensor", None),
            P(("groups", "tensor"), None, ("pool", "seq")),
        ),
        check_vma=False,
    )
```

```python
import functools

import jax
import jax.numpy as jnp
from jax import lax
from jax.experimental import pallas as pl
from jax.experimental.pallas import tpu as pltpu
from jax.sharding import PartitionSpec as P

EPSILON = 1e-06
THETA = 10000.0


MESH = pl.DeviceIdType.MESH


def tail_kernel(
    o_ref,
    lse_ref,
    absorb_ref,
    proj_ref,
    out_ref,
    o_in,
    lse_in,
    heads,
    up,
    down,
    total_ref,
    pair_send,
    pair_recv,
    gather_send,
    gather_recv,
    forward_send,
    forward_recv,
    up_send,
    up_recv,
    down_send,
    down_recv,
):
    tensor_count = lax.axis_size("tensor")
    pool_count = lax.axis_size("pool")
    depth = lax.axis_index("tensor")
    pool = lax.axis_index("pool")
    seq = lax.axis_index("seq")
    head_count, half, _ = o_ref.shape[1:]
    value_width = absorb_ref.shape[2]
    chunk = out_ref.shape[0]
    other = 1 - seq
    has_below = depth > 0
    has_above = depth < tensor_count - 1

    pair = [
        pltpu.make_async_remote_copy(
            src_ref=lse_ref.at[other],
            dst_ref=lse_in,
            send_sem=pair_send.at[0],
            recv_sem=pair_recv.at[0],
            device_id={"seq": other},
            device_id_type=MESH,
        )
    ] + [
        pltpu.make_async_remote_copy(
            src_ref=o_ref.at[other, h],
            dst_ref=o_in.at[h],
            send_sem=pair_send.at[1 + h],
            recv_sem=pair_recv.at[1 + h],
            device_id={"seq": other},
            device_id_type=MESH,
        )
        for h in range(head_count)
    ]
    for copy in pair:
        copy.start()
    own_rows = pl.ds(pl.multiple_of((pool * 2 + seq) * half, half), half)
    pair[0].wait_recv()
    for h in range(head_count):
        pair[1 + h].wait_recv()
        mine = lse_ref[seq, h][:, :1]
        theirs = lse_in[h][:, :1]
        ratio = 1.0 / (1.0 + jnp.exp(jnp.clip(theirs - mine, -80.0, 80.0)))
        merged = o_ref[seq, h].astype(jnp.float32) * ratio + o_in[h].astype(jnp.float32) * (
            1.0 - ratio
        )
        heads[own_rows, h * value_width : (h + 1) * value_width] = jnp.dot(
            merged.astype(jnp.bfloat16), absorb_ref[h], preferred_element_type=jnp.float32
        ).astype(jnp.bfloat16)

    def rows_of(pool_id, seq_id):
        return pl.ds(pl.multiple_of((pool_id * 2 + seq_id) * half, half), half)

    gathers = []
    for step in range(1, pool_count):
        gathers.append(
            pltpu.make_async_remote_copy(
                src_ref=heads.at[own_rows],
                dst_ref=heads.at[own_rows],
                send_sem=gather_send.at[step],
                recv_sem=gather_recv.at[step],
                device_id={"pool": lax.rem(pool + step, pool_count)},
                device_id_type=MESH,
            )
        )
    forwards = []
    for step in range(pool_count):
        rows = rows_of(lax.rem(pool + pool_count - step, pool_count), seq)
        forwards.append(
            pltpu.make_async_remote_copy(
                src_ref=heads.at[rows],
                dst_ref=heads.at[rows],
                send_sem=forward_send.at[step],
                recv_sem=forward_recv.at[step],
                device_id={"seq": other},
                device_id_type=MESH,
            )
        )
    for copy in gathers:
        copy.start()
    forwards[0].start()
    for step in range(1, pool_count):
        gathers[step - 1].wait_recv()
        forwards[step].start()
    for copy in forwards:
        copy.wait_recv()

    def project(dest):
        rows = pl.ds(pl.multiple_of(dest * chunk, chunk), chunk)
        return jnp.dot(heads[rows, :], proj_ref[...], preferred_element_type=jnp.float32)

    def lane_copy(buffer, send, recv, dest, target):
        return pltpu.make_async_remote_copy(
            src_ref=buffer.at[dest],
            dst_ref=buffer.at[dest],
            send_sem=send.at[dest],
            recv_sem=recv.at[dest],
            device_id={"tensor": target},
            device_id_type=MESH,
        )

    def pass_on(buffer, send, recv, dest, target, has_source):
        part = project(dest)
        copy = lane_copy(buffer, send, recv, dest, target)

        @pl.when(has_source)
        def _():
            copy.wait_recv()
            buffer[dest] = (buffer[dest].astype(jnp.float32) + part).astype(jnp.bfloat16)

        @pl.when(jnp.logical_not(has_source))
        def _():
            buffer[dest] = part.astype(jnp.bfloat16)

        copy.start()

    def turn(step, carry):
        high = tensor_count - 1 - step

        @pl.when(high > depth)
        def _():
            pass_on(up, up_send, up_recv, high, depth + 1, has_below)

        @pl.when(step < depth)
        def _():
            pass_on(down, down_send, down_recv, step, depth - 1, has_above)

        return carry

    lax.fori_loop(0, tensor_count - 1, turn, 0)
    total = project(depth)

    total_ref[...] = total

    @pl.when(has_below)
    def _():
        lane_copy(up, up_send, up_recv, depth, depth - 1).wait_recv()
        total_ref[...] += up[depth].astype(jnp.float32)

    @pl.when(has_above)
    def _():
        lane_copy(down, down_send, down_recv, depth, depth + 1).wait_recv()
        total_ref[...] += down[depth].astype(jnp.float32)

    out_ref[...] = total_ref[...].astype(jnp.bfloat16)

    def drain(step, carry):
        high = tensor_count - 1 - step

        @pl.when(high > depth)
        def _():
            lane_copy(up, up_send, up_recv, high, depth + 1).wait_send()

        @pl.when(step < depth)
        def _():
            lane_copy(down, down_send, down_recv, step, depth - 1).wait_send()

        return carry

    lax.fori_loop(0, tensor_count - 1, drain, 0)
    for copy in pair + gathers + forwards:
        copy.wait_send()


PAGE_BATCH = 8
NEG = -1e30


def dot_keys(query, keys):
    return lax.dot_general(
        query, keys, (((1,), (1,)), ((), ())), preferred_element_type=jnp.float32
    )


def front_kernel(
    scale,
    page_row_ref,
    row_page_ref,
    cache_len_ref,
    owner_ref,
    senders_ref,
    prompt_lens_ref,
    states_ref,
    down_ref,
    gain_ref,
    freq_ref,
    query_ref,
    steps_ref,
    cache_ref,
    new_ref,
    o_ref,
    lse_ref,
    outgoing,
    incoming,
    summed_ref,
    finished,
    pool_out,
    arrived,
    pages,
    page_o,
    page_top,
    page_total,
    page_sem,
    sum_send,
    sum_recv,
    new_send,
    new_recv,
    pool_send,
    pool_recv,
    all_send,
    all_recv,
):
    tensor_count = lax.axis_size("tensor")
    pool_count = lax.axis_size("pool")
    depth = lax.axis_index("tensor")
    pool = lax.axis_index("pool")
    sub = states_ref.shape[2]
    width = down_ref.shape[0]
    lat_width = gain_ref.shape[1]
    row_count, per_row, _ = query_ref.shape
    page_len = cache_ref.shape[2]
    seq = lax.axis_index("seq")
    seq_count = lax.axis_size("seq")
    batches = row_count // PAGE_BATCH
    span = tensor_count // 2

    def page_copy(index):
        return pltpu.make_async_copy(
            cache_ref.at[pl.ds(index * PAGE_BATCH, PAGE_BATCH)],
            pages.at[lax.rem(index, 2)],
            page_sem.at[lax.rem(index, 2)],
        )

    page_copy(jnp.int32(0)).start()
    barrier = pltpu.get_barrier_semaphore()
    for step in range(1, tensor_count):
        pl.semaphore_signal(
            barrier,
            inc=1,
            device_id={"tensor": lax.rem(depth + step, tensor_count)},
            device_id_type=MESH,
        )
    for step in range(1, pool_count):
        pl.semaphore_signal(
            barrier,
            inc=1,
            device_id={"pool": lax.rem(pool + step, pool_count)},
            device_id_type=MESH,
        )
    pl.semaphore_signal(barrier, inc=1, device_id={"seq": 1 - seq}, device_id_type=MESH)
    pl.semaphore_wait(barrier, tensor_count + pool_count - 1)

    def partial(dest):
        rows = states_ref[:, dest].reshape(2 * sub, states_ref.shape[3])
        return dot_keys(rows, down_ref[...])

    def sum_copy(step):
        return pltpu.make_async_remote_copy(
            src_ref=outgoing.at[step],
            dst_ref=incoming.at[step],
            send_sem=sum_send.at[step],
            recv_sem=sum_recv.at[step],
            device_id={"tensor": lax.rem(depth + step, tensor_count)},
            device_id_type=MESH,
        )

    def all_copy(step):
        return pltpu.make_async_remote_copy(
            src_ref=arrived.at[depth],
            dst_ref=arrived.at[depth],
            send_sem=all_send.at[step],
            recv_sem=all_recv.at[step],
            device_id={"tensor": lax.rem(depth + step, tensor_count)},
            device_id_type=MESH,
        )

    def pool_copy(step):
        target = lax.rem(pool + step, pool_count)
        return pltpu.make_async_remote_copy(
            src_ref=pool_out.at[target],
            dst_ref=arrived.at[depth, pool],
            send_sem=pool_send.at[step],
            recv_sem=pool_recv.at[step],
            device_id={"pool": target},
            device_id_type=MESH,
        )

    def new_copy(block):
        return pltpu.make_async_remote_copy(
            src_ref=finished.at[block],
            dst_ref=new_ref.at[lax.rem(depth, 2)],
            send_sem=new_send.at[block],
            recv_sem=new_recv.at[lax.rem(depth, 2)],
            device_id={"tensor": block * span + depth // 2},
            device_id_type=MESH,
        )

    def each(first, last, body):
        def run(step, carry):
            body(step)
            return carry

        lax.fori_loop(first, last, run, 0)

    def send_partial(step):
        outgoing[step] = partial(lax.rem(depth + step, tensor_count)).astype(jnp.bfloat16)
        sum_copy(step).start()

    each(1, tensor_count, send_partial)
    summed_ref[...] = partial(depth)

    def attend_batch(index):
        @pl.when(index + 1 < batches)
        def _():
            page_copy(index + 1).start()

        page_copy(index).wait()
        slot = lax.rem(index, 2)
        for item in range(PAGE_BATCH):
            page = index * PAGE_BATCH + item
            row = page_row_ref[page]
            query = query_ref[row]
            keys = pages[slot, item]
            scores = jnp.dot(query, keys, preferred_element_type=jnp.float32) * scale
            ids = lax.broadcasted_iota(jnp.int32, scores.shape, 1)
            valid = ids < cache_len_ref[pool * row_count + row] - seq * page_len
            scores = jnp.where(valid, scores, NEG)
            top = jnp.max(scores, axis=1, keepdims=True)
            weights = jnp.where(valid, jnp.exp(scores - top), 0.0)
            page_top[page] = jnp.broadcast_to(top, (per_row, 128))
            page_total[page] = jnp.broadcast_to(
                jnp.sum(weights, axis=1, keepdims=True), (per_row, 128)
            )
            page_o[page] = dot_keys(weights.astype(jnp.bfloat16), keys[:lat_width])

    first_stop = batches // 2
    second_stop = first_stop + max(batches // 8, 1)
    each(0, first_stop, attend_batch)

    each(1, tensor_count, lambda step: sum_copy(step).wait_recv())

    def add_partial(step):
        summed_ref[...] += incoming[step].astype(jnp.float32)

    each(1, tensor_count, add_partial)
    latent = summed_ref[:, :lat_width]
    rotary = summed_ref[:, lat_width:]
    half_width = (width - lat_width) // 2
    normed = (
        latent
        * lax.rsqrt(jnp.mean(latent * latent, axis=1, keepdims=True) + EPSILON)
        * gain_ref[...]
    )
    swapped = jnp.concatenate([rotary[:, half_width:], rotary[:, :half_width]], axis=1)
    line_ids = lax.broadcasted_iota(jnp.int32, (2 * sub, 1), 0)
    own_first = 2 * (pool * seq_count + seq)
    own_rows = [owner_ref[senders_ref[own_first + block]] for block in range(2)]
    bases = [cache_len_ref[row] for row in own_rows]
    positions = jnp.where(line_ids < sub, bases[0], bases[1]) + depth * sub + lax.rem(line_ids, sub)
    angles = positions.astype(jnp.float32) * freq_ref[...]
    lanes = lax.broadcasted_iota(jnp.int32, (1, 2 * half_width), 1)
    sine = jnp.where(lanes < half_width, -1.0, 1.0) * jnp.sin(angles)
    turned = rotary * jnp.cos(angles) + swapped * sine
    normed = normed.astype(jnp.bfloat16)
    turned = turned.astype(jnp.bfloat16)
    for block in range(2):
        finished[block, :, :lat_width] = normed[block * sub : (block + 1) * sub]
        finished[block, :, lat_width:] = turned[block * sub : (block + 1) * sub]

    def choose(target):
        first = own_rows[0] // row_count == target
        second = own_rows[1] // row_count == target
        none = jnp.zeros(finished.shape[1:], jnp.bfloat16)
        return jnp.where(first, finished[0], jnp.where(second, finished[1], none))

    def send_pool(step):
        target = lax.rem(pool + step, pool_count)
        pool_out[target] = choose(target)
        pool_copy(step).start()

    each(1, pool_count, send_pool)
    arrived[depth, pool] = choose(pool)
    for block in range(2):
        keep = block * span + depth // 2 == depth

        @pl.when(keep)
        def _(block=block):
            new_ref[lax.rem(depth, 2)] = finished[block]

    each(first_stop, second_stop, attend_batch)

    def pool_wait(step):
        pltpu.make_async_remote_copy(
            src_ref=pool_out.at[pool],
            dst_ref=arrived.at[depth, lax.rem(pool + pool_count - step, pool_count)],
            send_sem=pool_send.at[step],
            recv_sem=pool_recv.at[step],
            device_id={"pool": lax.rem(pool + step, pool_count)},
            device_id_type=MESH,
        ).wait_recv()

    each(1, pool_count, pool_wait)
    each(1, tensor_count, lambda step: all_copy(step).start())
    for block in range(2):

        @pl.when(block * span + depth // 2 != depth)
        def _(block=block):
            new_copy(block).start()

    each(second_stop, batches, attend_batch)

    def all_wait(step):
        source = lax.rem(depth + tensor_count - step, tensor_count)
        pltpu.make_async_remote_copy(
            src_ref=arrived.at[source],
            dst_ref=arrived.at[source],
            send_sem=all_send.at[step],
            recv_sem=all_recv.at[step],
            device_id={"tensor": source},
            device_id_type=MESH,
        ).wait_recv()

    each(1, tensor_count, all_wait)

    prompt_keys = tensor_count * pool_count * sub
    step_keys = steps_ref.shape[0]
    rows_in = 8
    lines = rows_in * per_row
    step_count = step_keys // row_count
    head_count = per_row // step_count
    groups = row_count // rows_in
    key_ids = lax.broadcasted_iota(jnp.int32, (1, prompt_keys), 1)
    key_pool = lax.rem(key_ids // sub, pool_count)
    key_slot = key_ids // (pool_count * sub) * sub + lax.rem(key_ids, sub)
    new_row = jnp.full((1, prompt_keys), -1, jnp.int32)
    for source in range(pool_count):
        for block in range(2):
            sender = 2 * (source * seq_count + seq) + block
            target = owner_ref[senders_ref[sender]]
            local_row = target - pool * row_count
            local_row = jnp.where((local_row >= 0) & (local_row < row_count), local_row, -1)
            hit = (key_pool == source) & (key_slot < prompt_lens_ref[sender]) & (local_row >= 0)
            new_row = jnp.where(hit, local_row, new_row)
    own_ids = lax.broadcasted_iota(jnp.int32, (1, step_keys), 1)
    own_row = jnp.where(seq == 0, own_ids // step_count, -1)
    own_step = lax.rem(own_ids, step_count)
    to_lines = lax.broadcasted_iota(jnp.int32, (lines, lines), 0)
    from_lines = lax.broadcasted_iota(jnp.int32, (lines, lines), 1)
    per_head = rows_in * step_count
    source_line = (
        lax.rem(to_lines // step_count, rows_in) * per_row
        + to_lines // per_head * step_count
        + lax.rem(to_lines, step_count)
    )
    permutation = (from_lines == source_line).astype(jnp.float32)

    def merge(group):
        query = query_ref[pl.ds(group * rows_in, rows_in)].reshape(lines, width)
        line_ids = lax.broadcasted_iota(jnp.int32, (lines, 1), 0)
        row_ids = group * rows_in + line_ids // per_row
        step_ids = lax.rem(line_ids, step_count)
        top = []
        total = []
        mixed = []
        for item in range(rows_in):
            page = row_page_ref[group * rows_in + item]
            top.append(page_top[page])
            total.append(page_total[page])
            mixed.append(page_o[page])
        top = jnp.concatenate(top, axis=0)[:, :1]
        total = jnp.concatenate(total, axis=0)[:, :1]
        mixed = jnp.concatenate(mixed, axis=0)
        prompts = arrived[...].reshape(prompt_keys, width)
        own = steps_ref[...]

        own_mask = (own_row == row_ids) & (own_step <= step_ids)
        new_mask = new_row == row_ids
        own_scores = jnp.where(own_mask, dot_keys(query, own) * scale, NEG)
        new_scores = jnp.where(new_mask, dot_keys(query, prompts) * scale, NEG)
        best = jnp.maximum(
            top,
            jnp.maximum(
                jnp.max(own_scores, axis=1, keepdims=True),
                jnp.max(new_scores, axis=1, keepdims=True),
            ),
        )
        own_weights = jnp.where(own_mask, jnp.exp(own_scores - best), 0.0)
        new_weights = jnp.where(new_mask, jnp.exp(new_scores - best), 0.0)
        old = jnp.exp(top - best)
        total = (
            total * old
            + jnp.sum(own_weights, axis=1, keepdims=True)
            + jnp.sum(new_weights, axis=1, keepdims=True)
        )
        mixed = (
            mixed * old
            + jnp.dot(
                own_weights.astype(jnp.bfloat16),
                own[:, :lat_width],
                preferred_element_type=jnp.float32,
            )
            + jnp.dot(
                new_weights.astype(jnp.bfloat16),
                prompts[:, :lat_width],
                preferred_element_type=jnp.float32,
            )
        )
        positive = total > 0.0
        safe = jnp.where(positive, total, 1.0)
        by_head = jnp.dot(
            permutation.astype(jnp.bfloat16),
            (mixed / safe).astype(jnp.bfloat16),
            preferred_element_type=jnp.float32,
        ).astype(jnp.bfloat16)
        lse = jnp.broadcast_to(jnp.where(positive, best + jnp.log(safe), NEG), (lines, 128))
        lse_by_head = jnp.dot(
            permutation, lse, precision=lax.Precision.HIGHEST, preferred_element_type=jnp.float32
        )
        part = group // (groups // 2)
        start = pl.multiple_of(lax.rem(group, groups // 2) * per_head, per_head)
        for head in range(head_count):
            taken = slice(head * per_head, (head + 1) * per_head)
            o_ref[part, head, pl.ds(start, per_head), :] = by_head[taken]
            lse_ref[part, head, pl.ds(start, per_head), :] = lse_by_head[taken]

    each(0, row_count // rows_in, merge)

    for slot in range(2):
        source = lax.rem(depth, span) * 2 + slot

        @pl.when(source != depth)
        def _(slot=slot, source=source):
            pltpu.make_async_remote_copy(
                src_ref=finished.at[0],
                dst_ref=new_ref.at[slot],
                send_sem=new_send.at[0],
                recv_sem=new_recv.at[slot],
                device_id={"tensor": source},
                device_id_type=MESH,
            ).wait_recv()

    for block in range(2):

        @pl.when(block * span + depth // 2 != depth)
        def _(block=block):
            new_copy(block).wait_send()

    each(1, tensor_count, lambda step: sum_copy(step).wait_send())
    each(1, tensor_count, lambda step: all_copy(step).wait_send())
    each(1, pool_count, lambda step: pool_copy(step).wait_send())


def whole_kernel(scale, scalar_count, array_count, front_scratch, *refs):
    inputs = scalar_count + array_count + 1
    front_inputs = refs[:inputs]
    absorb_ref, proj_ref, new_ref, out_ref, o_ref, lse_ref = refs[inputs : inputs + 6]
    scratch = refs[inputs + 6 :]
    front_kernel(scale, *front_inputs, new_ref, o_ref, lse_ref, *scratch[:front_scratch])
    tail_kernel(o_ref, lse_ref, absorb_ref, proj_ref, out_ref, *scratch[front_scratch:])


def fused(scale, scalars, arrays, cache_pages, value_absorb, out_proj):
    tensor_count = lax.axis_size("tensor")
    pool_count = lax.axis_size("pool")
    states, kv_down, kv_gain, _, queries, steps = arrays
    sub = states.shape[2]
    width = kv_down.shape[0]
    lat_width = kv_gain.shape[1]
    row_count, per_row, _ = queries.shape
    step_count = steps.shape[0] // row_count
    head_count = per_row // step_count
    half = row_count * step_count // 2
    columns = out_proj.shape[1]
    total_rows = pool_count * 2 * half
    chunk = total_rows // tensor_count
    vmem = pl.BlockSpec(memory_space=pltpu.VMEM)
    dma = pltpu.SemaphoreType.DMA
    front_scratch = [
        pltpu.VMEM((tensor_count, 2 * sub, width), jnp.bfloat16),
        pltpu.VMEM((tensor_count, 2 * sub, width), jnp.bfloat16),
        pltpu.VMEM((2 * sub, width), jnp.float32),
        pltpu.VMEM((2, sub, width), jnp.bfloat16),
        pltpu.VMEM((pool_count, sub, width), jnp.bfloat16),
        pltpu.VMEM((tensor_count, pool_count, sub, width), jnp.bfloat16),
        pltpu.VMEM((2, PAGE_BATCH) + cache_pages.shape[1:], jnp.bfloat16),
        pltpu.VMEM((row_count, per_row, lat_width), jnp.float32),
        pltpu.VMEM((row_count, per_row, 128), jnp.float32),
        pltpu.VMEM((row_count, per_row, 128), jnp.float32),
        dma((2,)),
        dma((tensor_count,)),
        dma((tensor_count,)),
        dma((2,)),
        dma((2,)),
        dma((pool_count,)),
        dma((pool_count,)),
        dma((tensor_count,)),
        dma((tensor_count,)),
    ]
    tail_scratch = [
        pltpu.VMEM((head_count, half, lat_width), jnp.bfloat16),
        pltpu.VMEM((head_count, half, 128), jnp.float32),
        pltpu.VMEM((total_rows, out_proj.shape[0]), jnp.bfloat16),
        pltpu.VMEM((tensor_count, chunk, columns), jnp.bfloat16),
        pltpu.VMEM((tensor_count, chunk, columns), jnp.bfloat16),
        pltpu.VMEM((chunk, columns), jnp.float32),
        dma((1 + head_count,)),
        dma((1 + head_count,)),
        dma((pool_count,)),
        dma((pool_count,)),
        dma((pool_count,)),
        dma((pool_count,)),
        dma((tensor_count,)),
        dma((tensor_count,)),
        dma((tensor_count,)),
        dma((tensor_count,)),
    ]
    return pl.pallas_call(
        functools.partial(
            whole_kernel, scale, len(scalars), len(arrays), len(front_scratch)
        ),
        out_shape=(
            jax.ShapeDtypeStruct((2, sub, width), jnp.bfloat16),
            jax.ShapeDtypeStruct((chunk, columns), jnp.bfloat16),
        ),
        in_specs=[pl.BlockSpec(memory_space=pltpu.SMEM)] * len(scalars)
        + [vmem] * len(arrays)
        + [pl.BlockSpec(memory_space=pl.ANY), vmem, vmem],
        out_specs=(vmem, vmem),
        scratch_shapes=[
            pltpu.VMEM((2, head_count, half, lat_width), jnp.bfloat16),
            pltpu.VMEM((2, head_count, half, 128), jnp.float32),
        ]
        + front_scratch
        + tail_scratch,
        compiler_params=pltpu.CompilerParams(
            collective_id=0, has_side_effects=True, vmem_limit_bytes=52 * 1024 * 1024
        ),
        name="fused",
    )(*scalars, *arrays, cache_pages, value_absorb, out_proj)


def local(
    prompt_states,
    kv_down,
    kv_gain,
    queries,
    step_latents,
    key_absorb,
    value_absorb,
    out_proj,
    cache_pages,
    page_table,
    cache_len,
    owner_map,
    senders,
    prompt_lens,
):
    tensor_count = lax.axis_size("tensor")
    sub = prompt_states.shape[1] // 2 // tensor_count
    row_count = queries.shape[0]
    lat_width = kv_gain.shape[0]
    width = kv_down.shape[1]
    head_count = key_absorb.shape[0]
    nope_width = key_absorb.shape[1]
    step_count = queries.shape[1]
    query_width = queries.shape[2] // head_count
    half_width = (width - lat_width) // 2
    inv_freq = THETA ** (-(jnp.arange(half_width, dtype=jnp.float32) * 2.0 / (2 * half_width)))
    page_ids = page_table[:, 0, 0]
    local_rows = jnp.arange(row_count, dtype=jnp.int32)
    matches = (page_ids[None, :] == local_rows[:, None]).astype(jnp.int32)
    page_rows = jnp.sum(matches * local_rows[None, :], axis=1)
    query_heads = queries.reshape(row_count, step_count, head_count, query_width)
    q_lat = jnp.einsum(
        "rshn,hnl->rhsl",
        query_heads[..., :nope_width],
        key_absorb,
        preferred_element_type=jnp.float32,
    ).astype(jnp.bfloat16)
    query_cat = jnp.concatenate(
        [q_lat, query_heads[..., nope_width:].transpose(0, 2, 1, 3)], axis=3
    ).reshape(row_count, head_count * step_count, width)
    new_pieces, attended = fused(
        float(query_width) ** (-0.5),
        (page_rows, page_ids, cache_len, owner_map, senders, prompt_lens),
        (
            prompt_states.reshape(2, tensor_count, sub, prompt_states.shape[2]),
            kv_down.T,
            kv_gain[None, :],
            jnp.concatenate([inv_freq, inv_freq])[None, :],
            query_cat,
            step_latents.reshape(row_count * step_count, width),
        ),
        cache_pages.transpose(0, 2, 1),
        value_absorb,
        out_proj,
    )
    new_latents = new_pieces.reshape(1, 2 * sub, width)
    attended = attended.reshape(-1, step_count, out_proj.shape[1])
    return (new_latents, attended)


def solution(mesh):
    placed = (
        P(("groups", "pool", "seq"), None, "tensor"),
        P("tensor", None),
        P(),
        P(("groups", "pool"), None, "tensor"),
        P(("groups", "pool"), None, None),
        P("tensor", None, None),
        P("tensor", None, None),
        P("tensor", ("pool", "seq")),
        P(("groups", "pool", "seq"), None, None),
        P(("groups", "pool"), "seq", None),
        P("groups"),
        P("groups"),
        P("groups"),
        P("groups"),
    )
    return jax.shard_map(
        local,
        mesh=mesh,
        in_specs=placed,
        out_specs=(
            P(("groups", "pool", "seq"), "tensor", None),
            P(("groups", "tensor"), None, ("pool", "seq")),
        ),
        check_vma=False,
    )
```

```python
import functools

import jax
import jax.numpy as jnp
from jax import lax
from jax.experimental import pallas as pl
from jax.experimental.pallas import tpu as pltpu
from jax.sharding import PartitionSpec as P

EPSILON = 1e-06
THETA = 10000.0


MESH = pl.DeviceIdType.MESH


def tail_kernel(
    o_ref,
    lse_ref,
    absorb_ref,
    proj_ref,
    out_ref,
    o_in,
    lse_in,
    heads,
    up,
    down,
    total_ref,
    pair_send,
    pair_recv,
    gather_send,
    gather_recv,
    forward_send,
    forward_recv,
    up_send,
    up_recv,
    down_send,
    down_recv,
):
    tensor_count = lax.axis_size("tensor")
    pool_count = lax.axis_size("pool")
    depth = lax.axis_index("tensor")
    pool = lax.axis_index("pool")
    seq = lax.axis_index("seq")
    head_count, half, _ = o_ref.shape[1:]
    value_width = absorb_ref.shape[2]
    chunk = out_ref.shape[0]
    other = 1 - seq
    has_below = depth > 0
    has_above = depth < tensor_count - 1

    pair = [
        pltpu.make_async_remote_copy(
            src_ref=lse_ref.at[other],
            dst_ref=lse_in,
            send_sem=pair_send.at[0],
            recv_sem=pair_recv.at[0],
            device_id={"seq": other},
            device_id_type=MESH,
        )
    ] + [
        pltpu.make_async_remote_copy(
            src_ref=o_ref.at[other, h],
            dst_ref=o_in.at[h],
            send_sem=pair_send.at[1 + h],
            recv_sem=pair_recv.at[1 + h],
            device_id={"seq": other},
            device_id_type=MESH,
        )
        for h in range(head_count)
    ]
    for copy in pair:
        copy.start()
    own_rows = pl.ds(pl.multiple_of((pool * 2 + seq) * half, half), half)
    pair[0].wait_recv()
    for h in range(head_count):
        pair[1 + h].wait_recv()
        mine = lse_ref[seq, h][:, :1]
        theirs = lse_in[h][:, :1]
        ratio = 1.0 / (1.0 + jnp.exp(jnp.clip(theirs - mine, -80.0, 80.0)))
        merged = o_ref[seq, h].astype(jnp.float32) * ratio + o_in[h].astype(jnp.float32) * (
            1.0 - ratio
        )
        heads[own_rows, h * value_width : (h + 1) * value_width] = jnp.dot(
            merged.astype(jnp.bfloat16), absorb_ref[h], preferred_element_type=jnp.float32
        ).astype(jnp.bfloat16)

    def rows_of(pool_id, seq_id):
        return pl.ds(pl.multiple_of((pool_id * 2 + seq_id) * half, half), half)

    gathers = []
    for step in range(1, pool_count):
        gathers.append(
            pltpu.make_async_remote_copy(
                src_ref=heads.at[own_rows],
                dst_ref=heads.at[own_rows],
                send_sem=gather_send.at[step],
                recv_sem=gather_recv.at[step],
                device_id={"pool": lax.rem(pool + step, pool_count)},
                device_id_type=MESH,
            )
        )
    forwards = []
    for step in range(pool_count):
        rows = rows_of(lax.rem(pool + pool_count - step, pool_count), seq)
        forwards.append(
            pltpu.make_async_remote_copy(
                src_ref=heads.at[rows],
                dst_ref=heads.at[rows],
                send_sem=forward_send.at[step],
                recv_sem=forward_recv.at[step],
                device_id={"seq": other},
                device_id_type=MESH,
            )
        )
    for copy in gathers:
        copy.start()
    forwards[0].start()
    for step in range(1, pool_count):
        gathers[step - 1].wait_recv()
        forwards[step].start()
    for copy in forwards:
        copy.wait_recv()

    def project(dest):
        rows = pl.ds(pl.multiple_of(dest * chunk, chunk), chunk)
        return jnp.dot(heads[rows, :], proj_ref[...], preferred_element_type=jnp.float32)

    def lane_copy(buffer, send, recv, dest, target):
        return pltpu.make_async_remote_copy(
            src_ref=buffer.at[dest],
            dst_ref=buffer.at[dest],
            send_sem=send.at[dest],
            recv_sem=recv.at[dest],
            device_id={"tensor": target},
            device_id_type=MESH,
        )

    def pass_on(buffer, send, recv, dest, target, has_source):
        part = project(dest)
        copy = lane_copy(buffer, send, recv, dest, target)

        @pl.when(has_source)
        def _():
            copy.wait_recv()
            buffer[dest] = (buffer[dest].astype(jnp.float32) + part).astype(jnp.bfloat16)

        @pl.when(jnp.logical_not(has_source))
        def _():
            buffer[dest] = part.astype(jnp.bfloat16)

        copy.start()

    def turn(step, carry):
        high = tensor_count - 1 - step

        @pl.when(high > depth)
        def _():
            pass_on(up, up_send, up_recv, high, depth + 1, has_below)

        @pl.when(step < depth)
        def _():
            pass_on(down, down_send, down_recv, step, depth - 1, has_above)

        return carry

    lax.fori_loop(0, tensor_count - 1, turn, 0)
    total = project(depth)

    total_ref[...] = total

    @pl.when(has_below)
    def _():
        lane_copy(up, up_send, up_recv, depth, depth - 1).wait_recv()
        total_ref[...] += up[depth].astype(jnp.float32)

    @pl.when(has_above)
    def _():
        lane_copy(down, down_send, down_recv, depth, depth + 1).wait_recv()
        total_ref[...] += down[depth].astype(jnp.float32)

    out_ref[...] = total_ref[...].astype(jnp.bfloat16)

    def drain(step, carry):
        high = tensor_count - 1 - step

        @pl.when(high > depth)
        def _():
            lane_copy(up, up_send, up_recv, high, depth + 1).wait_send()

        @pl.when(step < depth)
        def _():
            lane_copy(down, down_send, down_recv, step, depth - 1).wait_send()

        return carry

    lax.fori_loop(0, tensor_count - 1, drain, 0)
    for copy in pair + gathers + forwards:
        copy.wait_send()


PAGE_BATCH = 8
NEG = -1e30


def dot_keys(query, keys):
    return lax.dot_general(
        query, keys, (((1,), (1,)), ((), ())), preferred_element_type=jnp.float32
    )


def front_kernel(
    scale,
    page_row_ref,
    row_page_ref,
    cache_len_ref,
    owner_ref,
    senders_ref,
    prompt_lens_ref,
    states_ref,
    down_ref,
    gain_ref,
    freq_ref,
    query_ref,
    steps_ref,
    cache_ref,
    new_ref,
    o_ref,
    lse_ref,
    outgoing,
    incoming,
    summed_ref,
    finished,
    pool_out,
    arrived,
    asked,
    questions,
    reply_o,
    reply_lse,
    answer_o,
    answer_lse,
    pages,
    page_o,
    page_top,
    page_total,
    page_sem,
    sum_send,
    sum_recv,
    new_send,
    new_recv,
    pool_send,
    pool_recv,
    ask_send,
    ask_recv,
    reply_send,
    reply_recv,
    reply_lse_send,
    reply_lse_recv,
):
    tensor_count = lax.axis_size("tensor")
    pool_count = lax.axis_size("pool")
    depth = lax.axis_index("tensor")
    pool = lax.axis_index("pool")
    sub = states_ref.shape[2]
    width = down_ref.shape[0]
    lat_width = gain_ref.shape[1]
    row_count, per_row, _ = query_ref.shape
    page_len = cache_ref.shape[2]
    seq = lax.axis_index("seq")
    seq_count = lax.axis_size("seq")
    batches = row_count // PAGE_BATCH
    span = tensor_count // 2

    def page_copy(index):
        return pltpu.make_async_copy(
            cache_ref.at[pl.ds(index * PAGE_BATCH, PAGE_BATCH)],
            pages.at[lax.rem(index, 2)],
            page_sem.at[lax.rem(index, 2)],
        )

    page_copy(jnp.int32(0)).start()
    barrier = pltpu.get_barrier_semaphore()
    for step in range(1, tensor_count):
        pl.semaphore_signal(
            barrier,
            inc=1,
            device_id={"tensor": lax.rem(depth + step, tensor_count)},
            device_id_type=MESH,
        )
    for step in range(1, pool_count):
        pl.semaphore_signal(
            barrier,
            inc=1,
            device_id={"pool": lax.rem(pool + step, pool_count)},
            device_id_type=MESH,
        )
    pl.semaphore_signal(barrier, inc=1, device_id={"seq": 1 - seq}, device_id_type=MESH)
    pl.semaphore_wait(barrier, tensor_count + pool_count - 1)

    def partial(dest):
        rows = states_ref[:, dest].reshape(2 * sub, states_ref.shape[3])
        return dot_keys(rows, down_ref[...])

    def sum_copy(step):
        return pltpu.make_async_remote_copy(
            src_ref=outgoing.at[step],
            dst_ref=incoming.at[step],
            send_sem=sum_send.at[step],
            recv_sem=sum_recv.at[step],
            device_id={"tensor": lax.rem(depth + step, tensor_count)},
            device_id_type=MESH,
        )

    def peer(step):
        return lax.rem(depth + step, tensor_count)

    def ask_copy(step):
        return pltpu.make_async_remote_copy(
            src_ref=asked,
            dst_ref=questions.at[depth],
            send_sem=ask_send.at[step],
            recv_sem=ask_recv.at[step],
            device_id={"tensor": peer(step)},
            device_id_type=MESH,
        )

    def reply_copies(step):
        return [
            pltpu.make_async_remote_copy(
                src_ref=source.at[step],
                dst_ref=target.at[step],
                send_sem=send.at[step],
                recv_sem=recv.at[step],
                device_id={"tensor": peer(step)},
                device_id_type=MESH,
            )
            for source, target, send, recv in (
                (reply_o, answer_o, reply_send, reply_recv),
                (reply_lse, answer_lse, reply_lse_send, reply_lse_recv),
            )
        ]

    def pool_copy(step):
        target = lax.rem(pool + step, pool_count)
        return pltpu.make_async_remote_copy(
            src_ref=pool_out.at[target],
            dst_ref=arrived.at[pool],
            send_sem=pool_send.at[step],
            recv_sem=pool_recv.at[step],
            device_id={"pool": target},
            device_id_type=MESH,
        )

    def new_copy(block):
        return pltpu.make_async_remote_copy(
            src_ref=finished.at[block],
            dst_ref=new_ref.at[lax.rem(depth, 2)],
            send_sem=new_send.at[block],
            recv_sem=new_recv.at[lax.rem(depth, 2)],
            device_id={"tensor": block * span + depth // 2},
            device_id_type=MESH,
        )

    def each(first, last, body):
        def run(step, carry):
            body(step)
            return carry

        lax.fori_loop(first, last, run, 0)

    def send_partial(step):
        outgoing[step] = partial(lax.rem(depth + step, tensor_count)).astype(jnp.bfloat16)
        sum_copy(step).start()

    labels = []
    limits = []
    for source in range(pool_count):
        label = jnp.int32(-1)
        limit = jnp.int32(0)
        for block in range(2):
            sender = 2 * (source * seq_count + seq) + block
            local_row = owner_ref[senders_ref[sender]] - pool * row_count
            hit = (local_row >= 0) & (local_row < row_count)
            label = jnp.where(hit, local_row, label)
            limit = jnp.where(hit, prompt_lens_ref[sender], limit)
        labels.append(label)
        limits.append(limit)
        asked[source] = query_ref[jnp.maximum(label, 0)]
    questions[depth] = asked[...]
    each(1, tensor_count, lambda step: ask_copy(step).start())
    each(1, tensor_count, send_partial)
    summed_ref[...] = partial(depth)

    def attend_batch(index):
        @pl.when(index + 1 < batches)
        def _():
            page_copy(index + 1).start()

        page_copy(index).wait()
        slot = lax.rem(index, 2)
        for item in range(PAGE_BATCH):
            page = index * PAGE_BATCH + item
            row = page_row_ref[page]
            query = query_ref[row]
            keys = pages[slot, item]
            scores = jnp.dot(query, keys, preferred_element_type=jnp.float32) * scale
            ids = lax.broadcasted_iota(jnp.int32, scores.shape, 1)
            valid = ids < cache_len_ref[pool * row_count + row] - seq * page_len
            scores = jnp.where(valid, scores, NEG)
            top = jnp.max(scores, axis=1, keepdims=True)
            weights = jnp.where(valid, jnp.exp(scores - top), 0.0)
            page_top[page] = jnp.broadcast_to(top, (per_row, 128))
            page_total[page] = jnp.broadcast_to(
                jnp.sum(weights, axis=1, keepdims=True), (per_row, 128)
            )
            page_o[page] = dot_keys(weights.astype(jnp.bfloat16), keys[:lat_width])

    first_stop = batches // 2
    second_stop = first_stop + max(batches // 8, 1)
    each(0, first_stop, attend_batch)

    each(1, tensor_count, lambda step: sum_copy(step).wait_recv())

    def add_partial(step):
        summed_ref[...] += incoming[step].astype(jnp.float32)

    each(1, tensor_count, add_partial)
    latent = summed_ref[:, :lat_width]
    rotary = summed_ref[:, lat_width:]
    half_width = (width - lat_width) // 2
    normed = (
        latent
        * lax.rsqrt(jnp.mean(latent * latent, axis=1, keepdims=True) + EPSILON)
        * gain_ref[...]
    )
    swapped = jnp.concatenate([rotary[:, half_width:], rotary[:, :half_width]], axis=1)
    line_ids = lax.broadcasted_iota(jnp.int32, (2 * sub, 1), 0)
    own_first = 2 * (pool * seq_count + seq)
    own_rows = [owner_ref[senders_ref[own_first + block]] for block in range(2)]
    bases = [cache_len_ref[row] for row in own_rows]
    positions = jnp.where(line_ids < sub, bases[0], bases[1]) + depth * sub + lax.rem(line_ids, sub)
    angles = positions.astype(jnp.float32) * freq_ref[...]
    lanes = lax.broadcasted_iota(jnp.int32, (1, 2 * half_width), 1)
    sine = jnp.where(lanes < half_width, -1.0, 1.0) * jnp.sin(angles)
    turned = rotary * jnp.cos(angles) + swapped * sine
    normed = normed.astype(jnp.bfloat16)
    turned = turned.astype(jnp.bfloat16)
    for block in range(2):
        finished[block, :, :lat_width] = normed[block * sub : (block + 1) * sub]
        finished[block, :, lat_width:] = turned[block * sub : (block + 1) * sub]

    def choose(target):
        first = own_rows[0] // row_count == target
        second = own_rows[1] // row_count == target
        none = jnp.zeros(finished.shape[1:], jnp.bfloat16)
        return jnp.where(first, finished[0], jnp.where(second, finished[1], none))

    def send_pool(step):
        target = lax.rem(pool + step, pool_count)
        pool_out[target] = choose(target)
        pool_copy(step).start()

    each(1, pool_count, send_pool)
    arrived[pool] = choose(pool)
    for block in range(2):
        keep = block * span + depth // 2 == depth

        @pl.when(keep)
        def _(block=block):
            new_ref[lax.rem(depth, 2)] = finished[block]

    each(first_stop, second_stop, attend_batch)

    def pool_wait(step):
        pltpu.make_async_remote_copy(
            src_ref=pool_out.at[pool],
            dst_ref=arrived.at[lax.rem(pool + pool_count - step, pool_count)],
            send_sem=pool_send.at[step],
            recv_sem=pool_recv.at[step],
            device_id={"pool": lax.rem(pool + step, pool_count)},
            device_id_type=MESH,
        ).wait_recv()

    each(1, pool_count, pool_wait)

    def ask_wait(step):
        source = lax.rem(depth + tensor_count - step, tensor_count)
        pltpu.make_async_remote_copy(
            src_ref=asked,
            dst_ref=questions.at[source],
            send_sem=ask_send.at[step],
            recv_sem=ask_recv.at[step],
            device_id={"tensor": source},
            device_id_type=MESH,
        ).wait_recv()

    each(1, tensor_count, ask_wait)
    block_lines = pool_count * per_row
    block_keys = pool_count * sub

    def answer(target):
        query = questions[target].reshape(block_lines, width)
        keys = arrived[...].reshape(block_keys, width)
        scores = dot_keys(query, keys) * scale
        key_ids = lax.broadcasted_iota(jnp.int32, (1, block_keys), 1)
        query_ids = lax.broadcasted_iota(jnp.int32, (block_lines, 1), 0)
        key_limit = jnp.zeros((1, block_keys), jnp.int32)
        for source in range(pool_count):
            key_limit = jnp.where(key_ids // sub == source, limits[source], key_limit)
        valid = (key_ids // sub == query_ids // per_row) & (
            depth * sub + lax.rem(key_ids, sub) < key_limit
        )
        scores = jnp.where(valid, scores, NEG)
        top = jnp.max(scores, axis=1, keepdims=True)
        weights = jnp.where(valid, jnp.exp(scores - top), 0.0)
        total = jnp.sum(weights, axis=1, keepdims=True)
        mixed = jnp.dot(
            weights.astype(jnp.bfloat16), keys[:, :lat_width], preferred_element_type=jnp.float32
        )
        positive = total > 0.0
        safe = jnp.where(positive, total, 1.0)
        lse = jnp.where(positive, top + jnp.log(safe), NEG)
        return (mixed / safe).astype(jnp.bfloat16), jnp.broadcast_to(lse, (block_lines, 128))

    def send_answer(step):
        part, lse = answer(peer(step))
        reply_o[step] = part
        reply_lse[step] = lse
        for copy in reply_copies(step):
            copy.start()

    each(1, tensor_count, send_answer)
    own_part, own_lse = answer(depth)
    answer_o[0] = own_part
    answer_lse[0] = own_lse
    for block in range(2):

        @pl.when(block * span + depth // 2 != depth)
        def _(block=block):
            new_copy(block).start()

    each(second_stop, batches, attend_batch)

    def reply_wait(step):
        for copy in reply_copies(step):
            copy.wait_recv()

    each(1, tensor_count, reply_wait)
    block_top = answer_lse[0][:, :1]
    for step in range(1, tensor_count):
        block_top = jnp.maximum(block_top, answer_lse[step][:, :1])
    block_total = jnp.zeros((block_lines, 1), jnp.float32)
    block_mixed = jnp.zeros((block_lines, lat_width), jnp.float32)
    for step in range(tensor_count):
        share = jnp.exp(answer_lse[step][:, :1] - block_top)
        block_total = block_total + share
        block_mixed = block_mixed + share * answer_o[step].astype(jnp.float32)

    step_keys = steps_ref.shape[0]
    rows_in = 8
    lines = rows_in * per_row
    step_count = step_keys // row_count
    head_count = per_row // step_count
    groups = row_count // rows_in
    own_ids = lax.broadcasted_iota(jnp.int32, (1, step_keys), 1)
    own_row = jnp.where(seq == 0, own_ids // step_count, -1)
    own_step = lax.rem(own_ids, step_count)
    to_lines = lax.broadcasted_iota(jnp.int32, (lines, lines), 0)
    from_lines = lax.broadcasted_iota(jnp.int32, (lines, lines), 1)
    per_head = rows_in * step_count
    source_line = (
        lax.rem(to_lines // step_count, rows_in) * per_row
        + to_lines // per_head * step_count
        + lax.rem(to_lines, step_count)
    )
    permutation = (from_lines == source_line).astype(jnp.float32)

    def merge(group):
        query = query_ref[pl.ds(group * rows_in, rows_in)].reshape(lines, width)
        line_ids = lax.broadcasted_iota(jnp.int32, (lines, 1), 0)
        row_ids = group * rows_in + line_ids // per_row
        step_ids = lax.rem(line_ids, step_count)
        top = []
        total = []
        mixed = []
        for item in range(rows_in):
            page = row_page_ref[group * rows_in + item]
            top.append(page_top[page])
            total.append(page_total[page])
            mixed.append(page_o[page])
        top = jnp.concatenate(top, axis=0)[:, :1]
        total = jnp.concatenate(total, axis=0)[:, :1]
        mixed = jnp.concatenate(mixed, axis=0)
        own = steps_ref[...]

        own_mask = (own_row == row_ids) & (own_step <= step_ids)
        own_scores = jnp.where(own_mask, dot_keys(query, own) * scale, NEG)
        best = jnp.maximum(top, jnp.max(own_scores, axis=1, keepdims=True))
        extras = []
        for source in range(pool_count):
            taken = slice(source * per_row, (source + 1) * per_row)
            chosen = row_ids == labels[source]
            line_top, line_total, line_mixed = (
                jnp.concatenate([part[taken]] * rows_in, axis=0)
                for part in (block_top, block_total, block_mixed)
            )
            line_top = jnp.where(chosen, line_top, NEG)
            extras.append((chosen, line_top, line_total, line_mixed))
            best = jnp.maximum(best, line_top)
        own_weights = jnp.where(own_mask, jnp.exp(own_scores - best), 0.0)
        old = jnp.exp(top - best)
        total = total * old + jnp.sum(own_weights, axis=1, keepdims=True)
        mixed = mixed * old + jnp.dot(
            own_weights.astype(jnp.bfloat16),
            own[:, :lat_width],
            preferred_element_type=jnp.float32,
        )
        for chosen, line_top, line_total, line_mixed in extras:
            share = jnp.where(chosen, jnp.exp(line_top - best), 0.0)
            total = total + share * line_total
            mixed = mixed + share * line_mixed
        positive = total > 0.0
        safe = jnp.where(positive, total, 1.0)
        by_head = jnp.dot(
            permutation.astype(jnp.bfloat16),
            (mixed / safe).astype(jnp.bfloat16),
            preferred_element_type=jnp.float32,
        ).astype(jnp.bfloat16)
        lse = jnp.broadcast_to(jnp.where(positive, best + jnp.log(safe), NEG), (lines, 128))
        lse_by_head = jnp.dot(
            permutation, lse, precision=lax.Precision.HIGHEST, preferred_element_type=jnp.float32
        )
        part = group // (groups // 2)
        start = pl.multiple_of(lax.rem(group, groups // 2) * per_head, per_head)
        for head in range(head_count):
            taken = slice(head * per_head, (head + 1) * per_head)
            o_ref[part, head, pl.ds(start, per_head), :] = by_head[taken]
            lse_ref[part, head, pl.ds(start, per_head), :] = lse_by_head[taken]

    each(0, row_count // rows_in, merge)

    for slot in range(2):
        source = lax.rem(depth, span) * 2 + slot

        @pl.when(source != depth)
        def _(slot=slot, source=source):
            pltpu.make_async_remote_copy(
                src_ref=finished.at[0],
                dst_ref=new_ref.at[slot],
                send_sem=new_send.at[0],
                recv_sem=new_recv.at[slot],
                device_id={"tensor": source},
                device_id_type=MESH,
            ).wait_recv()

    for block in range(2):

        @pl.when(block * span + depth // 2 != depth)
        def _(block=block):
            new_copy(block).wait_send()

    each(1, tensor_count, lambda step: sum_copy(step).wait_send())
    each(1, tensor_count, lambda step: ask_copy(step).wait_send())

    def reply_drain(step):
        for copy in reply_copies(step):
            copy.wait_send()

    each(1, tensor_count, reply_drain)
    each(1, pool_count, lambda step: pool_copy(step).wait_send())


def whole_kernel(scale, scalar_count, array_count, front_scratch, *refs):
    inputs = scalar_count + array_count + 1
    front_inputs = refs[:inputs]
    absorb_ref, proj_ref, new_ref, out_ref, o_ref, lse_ref = refs[inputs : inputs + 6]
    scratch = refs[inputs + 6 :]
    front_kernel(scale, *front_inputs, new_ref, o_ref, lse_ref, *scratch[:front_scratch])
    tail_kernel(o_ref, lse_ref, absorb_ref, proj_ref, out_ref, *scratch[front_scratch:])


def fused(scale, scalars, arrays, cache_pages, value_absorb, out_proj):
    tensor_count = lax.axis_size("tensor")
    pool_count = lax.axis_size("pool")
    states, kv_down, kv_gain, _, queries, steps = arrays
    sub = states.shape[2]
    width = kv_down.shape[0]
    lat_width = kv_gain.shape[1]
    row_count, per_row, _ = queries.shape
    step_count = steps.shape[0] // row_count
    head_count = per_row // step_count
    half = row_count * step_count // 2
    columns = out_proj.shape[1]
    total_rows = pool_count * 2 * half
    chunk = total_rows // tensor_count
    vmem = pl.BlockSpec(memory_space=pltpu.VMEM)
    dma = pltpu.SemaphoreType.DMA
    front_scratch = [
        pltpu.VMEM((tensor_count, 2 * sub, width), jnp.bfloat16),
        pltpu.VMEM((tensor_count, 2 * sub, width), jnp.bfloat16),
        pltpu.VMEM((2 * sub, width), jnp.float32),
        pltpu.VMEM((2, sub, width), jnp.bfloat16),
        pltpu.VMEM((pool_count, sub, width), jnp.bfloat16),
        pltpu.VMEM((pool_count, sub, width), jnp.bfloat16),
        pltpu.VMEM((pool_count, per_row, width), jnp.bfloat16),
        pltpu.VMEM((tensor_count, pool_count, per_row, width), jnp.bfloat16),
        pltpu.VMEM((tensor_count, pool_count * per_row, lat_width), jnp.bfloat16),
        pltpu.VMEM((tensor_count, pool_count * per_row, 128), jnp.float32),
        pltpu.VMEM((tensor_count, pool_count * per_row, lat_width), jnp.bfloat16),
        pltpu.VMEM((tensor_count, pool_count * per_row, 128), jnp.float32),
        pltpu.VMEM((2, PAGE_BATCH) + cache_pages.shape[1:], jnp.bfloat16),
        pltpu.VMEM((row_count, per_row, lat_width), jnp.float32),
        pltpu.VMEM((row_count, per_row, 128), jnp.float32),
        pltpu.VMEM((row_count, per_row, 128), jnp.float32),
        dma((2,)),
        dma((tensor_count,)),
        dma((tensor_count,)),
        dma((2,)),
        dma((2,)),
        dma((pool_count,)),
        dma((pool_count,)),
        dma((tensor_count,)),
        dma((tensor_count,)),
        dma((tensor_count,)),
        dma((tensor_count,)),
        dma((tensor_count,)),
        dma((tensor_count,)),
    ]
    tail_scratch = [
        pltpu.VMEM((head_count, half, lat_width), jnp.bfloat16),
        pltpu.VMEM((head_count, half, 128), jnp.float32),
        pltpu.VMEM((total_rows, out_proj.shape[0]), jnp.bfloat16),
        pltpu.VMEM((tensor_count, chunk, columns), jnp.bfloat16),
        pltpu.VMEM((tensor_count, chunk, columns), jnp.bfloat16),
        pltpu.VMEM((chunk, columns), jnp.float32),
        dma((1 + head_count,)),
        dma((1 + head_count,)),
        dma((pool_count,)),
        dma((pool_count,)),
        dma((pool_count,)),
        dma((pool_count,)),
        dma((tensor_count,)),
        dma((tensor_count,)),
        dma((tensor_count,)),
        dma((tensor_count,)),
    ]
    return pl.pallas_call(
        functools.partial(
            whole_kernel, scale, len(scalars), len(arrays), len(front_scratch)
        ),
        out_shape=(
            jax.ShapeDtypeStruct((2, sub, width), jnp.bfloat16),
            jax.ShapeDtypeStruct((chunk, columns), jnp.bfloat16),
        ),
        in_specs=[pl.BlockSpec(memory_space=pltpu.SMEM)] * len(scalars)
        + [vmem] * len(arrays)
        + [pl.BlockSpec(memory_space=pl.ANY), vmem, vmem],
        out_specs=(vmem, vmem),
        scratch_shapes=[
            pltpu.VMEM((2, head_count, half, lat_width), jnp.bfloat16),
            pltpu.VMEM((2, head_count, half, 128), jnp.float32),
        ]
        + front_scratch
        + tail_scratch,
        compiler_params=pltpu.CompilerParams(
            collective_id=0, has_side_effects=True, vmem_limit_bytes=52 * 1024 * 1024
        ),
        name="fused",
    )(*scalars, *arrays, cache_pages, value_absorb, out_proj)


def local(
    prompt_states,
    kv_down,
    kv_gain,
    queries,
    step_latents,
    key_absorb,
    value_absorb,
    out_proj,
    cache_pages,
    page_table,
    cache_len,
    owner_map,
    senders,
    prompt_lens,
):
    tensor_count = lax.axis_size("tensor")
    sub = prompt_states.shape[1] // 2 // tensor_count
    row_count = queries.shape[0]
    lat_width = kv_gain.shape[0]
    width = kv_down.shape[1]
    head_count = key_absorb.shape[0]
    nope_width = key_absorb.shape[1]
    step_count = queries.shape[1]
    query_width = queries.shape[2] // head_count
    half_width = (width - lat_width) // 2
    inv_freq = THETA ** (-(jnp.arange(half_width, dtype=jnp.float32) * 2.0 / (2 * half_width)))
    page_ids = page_table[:, 0, 0]
    local_rows = jnp.arange(row_count, dtype=jnp.int32)
    matches = (page_ids[None, :] == local_rows[:, None]).astype(jnp.int32)
    page_rows = jnp.sum(matches * local_rows[None, :], axis=1)
    query_heads = queries.reshape(row_count, step_count, head_count, query_width)
    q_lat = jnp.einsum(
        "rshn,hnl->rhsl",
        query_heads[..., :nope_width],
        key_absorb,
        preferred_element_type=jnp.float32,
    ).astype(jnp.bfloat16)
    query_cat = jnp.concatenate(
        [q_lat, query_heads[..., nope_width:].transpose(0, 2, 1, 3)], axis=3
    ).reshape(row_count, head_count * step_count, width)
    new_pieces, attended = fused(
        float(query_width) ** (-0.5),
        (page_rows, page_ids, cache_len, owner_map, senders, prompt_lens),
        (
            prompt_states.reshape(2, tensor_count, sub, prompt_states.shape[2]),
            kv_down.T,
            kv_gain[None, :],
            jnp.concatenate([inv_freq, inv_freq])[None, :],
            query_cat,
            step_latents.reshape(row_count * step_count, width),
        ),
        cache_pages.transpose(0, 2, 1),
        value_absorb,
        out_proj,
    )
    new_latents = new_pieces.reshape(1, 2 * sub, width)
    attended = attended.reshape(-1, step_count, out_proj.shape[1])
    return (new_latents, attended)


def solution(mesh):
    placed = (
        P(("groups", "pool", "seq"), None, "tensor"),
        P("tensor", None),
        P(),
        P(("groups", "pool"), None, "tensor"),
        P(("groups", "pool"), None, None),
        P("tensor", None, None),
        P("tensor", None, None),
        P("tensor", ("pool", "seq")),
        P(("groups", "pool", "seq"), None, None),
        P(("groups", "pool"), "seq", None),
        P("groups"),
        P("groups"),
        P("groups"),
        P("groups"),
    )
    return jax.shard_map(
        local,
        mesh=mesh,
        in_specs=placed,
        out_specs=(
            P(("groups", "pool", "seq"), "tensor", None),
            P(("groups", "tensor"), None, ("pool", "seq")),
        ),
        check_vma=False,
    )
```
